256 devices in a mesh: ctx: 32 (over x, y, core), head: 8 (over z).
Axes of the slice: x: 4, y: 4, z: 8, core: 2. Of those that a mesh axis runs over, the one named last changes fastest.
Arguments:
- queries: bfloat16 [8192, 64, 128], P('ctx', 'head'), may hold values from -130 to 130
- keys: bfloat16 [8192, 8, 128], P(('ctx', 'head')), may hold values from -5 to 5
- values: bfloat16 [8192, 8, 128], P(('ctx', 'head')), may hold values from -5 to 5
- output: bfloat16 [8192, 64, 128], P('ctx', 'head'), may hold values from -5 to 5
- grad_output: bfloat16 [8192, 64, 128], P('ctx', 'head'), may hold values from -5 to 5
- doc_lengths: int32 [16], replicated, may hold values from 1 to 1024, 8192 in all
Outputs:
- grad_queries: bfloat16 [8192, 64, 128], P('ctx', 'head')
- grad_keys: bfloat16 [8192, 8, 128], P(('ctx', 'head'))
- grad_values: bfloat16 [8192, 8, 128], P(('ctx', 'head'))
The draws below stay inside these ranges and needn't reach their ends.
Inputs may be any that keep to these rules, and one draw needn't show every extreme that they name: `doc_lengths`: 16 positive lengths summing to 8192; the longest is exactly 1024.
All inputs are finite; a program needn't handle non-finite values.
Results may differ from the reference program's by a relative error of at most 0.0085.
Values may be sent and summed in bfloat16 or wider, within the bound.
A program may use at most 64 MiB of HBM per device.

```python
import math
import jax
import jax.numpy as jnp
import numpy as np
from jax import lax

QH = 64
KVH = 8
DH = 128
T_DEV = 256
REACH = 4
NDOCS = 16
TOKENS = 8192
MAXDOC = 1024
N_CTX = 32


def key_base(key):
    field = jax.random.normal(jax.random.fold_in(key, 101), (TOKENS, KVH, DH), jnp.float32)
    return jnp.clip(field, -5.0, 5.0)


def draw_keys(key, part):
    field = key_base(key)
    return field.astype(jnp.bfloat16)


def draw_queries(key, part):
    key = jax.random.fold_in(key, 7)
    result = jnp.clip(jax.random.normal(key, (TOKENS, QH, DH), jnp.float32), -5.0, 5.0)
    return result.astype(jnp.bfloat16)


def level_of(rng, dims, split, smallest, top_value):
    def one(dim, shards_of):
        draws = jax.random.uniform(jax.random.fold_in(jax.random.fold_in(rng, 6), dim), (shards_of,), jnp.float32, smallest / len(split), top_value / len(split))
        return jnp.repeat(jnp.exp(draws), dims[dim] // shards_of).reshape((-1,) + (1,) * (len(dims) - dim - 1))

    factor_of = one(*split[0])
    for cut in split[1:]:
        factor_of = factor_of * one(*cut)
    return factor_of


def split_up(amount, total, limit, lean):
    loads = [(1 << 20) // math.isqrt(grade ** lean) + 1 for grade in range(2, amount + 1)]
    spare, counts = total - limit - (amount - 1), [1] * (amount - 1)
    while spare > 0:
        movable = [i for i in range(amount - 1) if counts[i] < limit]
        pool, left = sum([loads[i] for i in movable]), spare
        for i in movable:
            extra = min(limit - counts[i], max(1, left * loads[i] // pool), spare)
            counts[i] = counts[i] + extra
            spare = spare - extra
    return np.array([limit] + counts)


def ragged(key, count, total, bound, skew):
    if count == 2:
        one = jax.random.randint(key, (), max(1, total - bound), min(bound, total - 1) + 1)
        return jnp.stack([one, total - one])
    lengths = jnp.asarray(split_up(count, total, bound, skew), jnp.int32)
    twos = (count - 1) // 2
    source_of, taker = lengths[1:1 + 2 * twos:2], lengths[2:2 + 2 * twos:2]
    slack = jnp.minimum(source_of - 1, bound - taker)
    shifted = jax.random.randint(jax.random.fold_in(key, 1), (twos,), 0, 1 << 20) % (slack + 1)
    lengths = lengths.at[1:1 + 2 * twos:2].set(source_of - shifted).at[2:2 + 2 * twos:2].set(taker + shifted)
    return lengths[jax.random.permutation(jax.random.fold_in(key, 2), count)]


def centred(rng, dims, deviation, limit, split=(), kind=jnp.bfloat16):
    array = jax.random.normal(rng, dims, jnp.float32) * deviation
    if len(split) > 0:
        array = level_of(rng, dims, split, -0.22, 0.18) * array
    return jnp.clip(array, min=-limit, max=limit).astype(kind)


def setup_inputs(seed: int = 0) -> dict:
    key_list = jax.random.split(jax.random.key(seed), 7)
    return {
        "queries": draw_queries(jax.random.fold_in(key_list[6], 71), 0),
        "keys": draw_keys(jax.random.fold_in(key_list[6], 71), 0),
        "values": centred(key_list[2], (TOKENS, KVH, DH), 1.0, 5.0, ((0, 256),)),
        "output": centred(key_list[3], (TOKENS, QH, DH), 1.0, 5.0, ((0, 32), (1, 8))),
        "grad_output": centred(key_list[4], (TOKENS, QH, DH), 1.0, 5.0, ((0, 32), (1, 8))),
        "doc_lengths": ragged(key_list[5], NDOCS, TOKENS, MAXDOC, 2).astype(jnp.int32),
    }


def segment_of(doc_lengths, positions):
    ends = jnp.cumsum(doc_lengths).astype(jnp.int32)
    return jnp.sum((ends[None, :] <= positions[:, None]).astype(jnp.int32), axis=1)


def reference(queries, keys, values, output, grad_output, doc_lengths):
    softmax_scale = 1.0 / (DH ** 0.5)
    groups = QH // KVH
    margin = REACH * T_DEV
    window = (REACH + 1) * T_DEV
    positions = jnp.arange(TOKENS, dtype=jnp.int32)
    segment = segment_of(doc_lengths, positions)
    pad_positions = jnp.arange(-margin, TOKENS, dtype=jnp.int32)
    filler_document_label = jnp.concatenate([jnp.full((margin,), -1, jnp.int32), segment])
    zero_rows = jnp.zeros((margin, KVH, DH), jnp.bfloat16)
    pad_keys = jnp.concatenate([zero_rows, keys], axis=0)
    pad_values = jnp.concatenate([zero_rows, values], axis=0)

    def one_block(carry, block):
        acc_keys, acc_values = carry
        start = (block * T_DEV).astype(jnp.int32)
        asking_portion = lax.dynamic_slice_in_dim(queries, start, T_DEV, 0).reshape(T_DEV, KVH, groups, DH).astype(jnp.float32)
        derivative_portion = lax.dynamic_slice_in_dim(grad_output, start, T_DEV, 0).reshape(T_DEV, KVH, groups, DH).astype(jnp.float32)
        output_slice = lax.dynamic_slice_in_dim(output, start, T_DEV, 0).reshape(T_DEV, KVH, groups, DH).astype(jnp.float32)
        key_slice = lax.dynamic_slice_in_dim(pad_keys, start, window, 0).astype(jnp.float32)
        value_slice = lax.dynamic_slice_in_dim(pad_values, start, window, 0).astype(jnp.float32)
        query_pos = lax.dynamic_slice_in_dim(positions, start, T_DEV, 0)
        asking_document_label = lax.dynamic_slice_in_dim(segment, start, T_DEV, 0)
        key_pos = lax.dynamic_slice_in_dim(pad_positions, start, window, 0)
        key_seg = lax.dynamic_slice_in_dim(filler_document_label, start, window, 0)
        allowed = (asking_document_label[:, None] == key_seg[None, :]) & (key_pos[None, :] <= query_pos[:, None]) & (key_pos[None, :] >= 0)
        logit_matrix = jnp.einsum("expu,axu->xpea", asking_portion, key_slice) * softmax_scale
        logit_matrix = jnp.where(allowed, logit_matrix, -1e30)
        top = jnp.max(logit_matrix, axis=-1)
        row_lse = top + jnp.log(jnp.sum(jnp.exp(logit_matrix - top[..., None]), axis=-1))
        probs = jnp.where(allowed, jnp.exp(logit_matrix - row_lse[..., None]), 0.0)
        attention_weights_lowprec = probs.astype(jnp.bfloat16).astype(jnp.float32)
        row_correction = jnp.einsum("epvx,epvx->pve", derivative_portion, output_slice)
        content_derivative = jnp.einsum("dapg,pdaf->gdf", attention_weights_lowprec, derivative_portion)
        probability_gradient = jnp.einsum("expu,axu->xpea", derivative_portion, value_slice)
        similarity_derivative = (probs * (probability_gradient - row_correction[..., None])).astype(jnp.bfloat16).astype(jnp.float32)
        query_gradient = (jnp.einsum("mlwp,pmz->wmlz", similarity_derivative, key_slice) * softmax_scale).astype(jnp.bfloat16)
        lookup_derivative_portion = jnp.einsum("dapg,pdaf->gdf", similarity_derivative, asking_portion)
        acc_keys = lax.dynamic_update_slice_in_dim(acc_keys, lax.dynamic_slice_in_dim(acc_keys, start, window, 0) + lookup_derivative_portion, start, 0)
        acc_values = lax.dynamic_update_slice_in_dim(acc_values, lax.dynamic_slice_in_dim(acc_values, start, window, 0) + content_derivative, start, 0)
        return (acc_keys, acc_values), query_gradient.reshape(T_DEV, QH, DH)

    empty = jnp.zeros((TOKENS + margin, KVH, DH), jnp.float32)
    (acc_keys, acc_values), grad_blocks = lax.scan(one_block, (empty, empty), jnp.arange(N_CTX, dtype=jnp.int32))
    grad_queries = grad_blocks.reshape(TOKENS, QH, DH)
    grad_keys = (acc_keys[margin:] * softmax_scale).astype(jnp.bfloat16)
    grad_values = acc_values[margin:].astype(jnp.bfloat16)
    return grad_queries, grad_keys, grad_values
```

```python
import functools
import math

import jax
import jax.numpy as jnp
from jax import lax
from jax.experimental import pallas as pl
from jax.experimental.pallas import tpu as pltpu
from jax.sharding import PartitionSpec as P

MESH = pl.DeviceIdType.MESH
F32 = jnp.float32
BF16 = jnp.bfloat16

BLOCK = 256
REACH = 4
WINDOW = (REACH + 1) * BLOCK
WIDTH = 128
HEADS = 8
GROUPS = 8
ROWS = BLOCK * HEADS
TILE = 256
TILES = ROWS // TILE
STEP = TILE // HEADS
BAND = REACH * BLOCK + STEP
PIECE = BLOCK // GROUPS
NDOCS = 16
FAR = 2.0**20
SCALE = 1.0 / math.sqrt(WIDTH)
RATE = SCALE / math.log(2.0)

CHUNKS = ((0, BLOCK), (BLOCK, BLOCK), (2 * BLOCK, BLOCK), (3 * BLOCK, BLOCK + STEP))

NT = (((1,), (1,)), ((), ()))
NN = (((1,), (0,)), ((), ()))
TN = (((0,), (0,)), ((), ()))


def dot(a, b, dims=NN):
    return lax.dot_general(a, b, dims, preferred_element_type=F32)


def iota(shape, dim):
    return lax.broadcasted_iota(jnp.int32, shape, dim)


def kernel(
    n_ctx,
    lens_ref, q_ref, o_ref, g_ref, k_ref, v_ref,
    dq_ref, dk_ref, dv_ref,
    kb, vb, kp, vp, kaug, qaug, gt, delta, band, m_st, l_st, w_st, wd_st,
    dka, dva, stage, got, fin, sent,
    ks_sem, kr_sem, vs_sem, vr_sem, cs_sem, cr_sem, rs_sem, rr_sem, fs_sem, fr_sem,
):
    c = lax.axis_index("ctx")
    z = lax.axis_index("head")
    core = lax.rem(c, 2)
    sib = c + 1 - 2 * core
    nxt = lax.rem(c + 2, n_ctx)
    prv = lax.rem(c + n_ctx - 2, n_ctx)
    peers = [lax.rem(z + o, GROUPS) for o in range(1, GROUPS)]

    barrier = pltpu.get_barrier_semaphore()
    for peer in peers:
        pl.semaphore_signal(barrier, inc=1, device_id={"head": peer}, device_id_type=MESH)
    for other in (sib, nxt, prv):
        pl.semaphore_signal(barrier, inc=1, device_id={"ctx": other}, device_id_type=MESH)

    row, col = iota((BLOCK, BLOCK), 0), iota((BLOCK, BLOCK), 1)
    order = jnp.where(
        col == (row % PIECE) * GROUPS + row // PIECE, 1.0, 0.0
    ).astype(BF16)
    kp[...] = dot(order, k_ref[...]).astype(BF16)
    vp[...] = dot(order, v_ref[...]).astype(BF16)

    pl.semaphore_wait(barrier, GROUPS + 2)

    mine = pl.multiple_of(PIECE * z, PIECE)
    k_copies, v_copies = [], []
    for piece, window, send, recv, copies in (
        (kp, kb, ks_sem, kr_sem, k_copies),
        (vp, vb, vs_sem, vr_sem, v_copies),
    ):
        for o, peer in enumerate(peers):
            copy = pltpu.make_async_remote_copy(
                src_ref=piece.at[pl.ds(pl.multiple_of(PIECE * peer, PIECE), PIECE)],
                dst_ref=window.at[pl.ds(pl.multiple_of(REACH * BLOCK + mine, PIECE), PIECE)],
                send_sem=send.at[o],
                recv_sem=recv.at[o],
                device_id={"head": peer},
                device_id_type=MESH,
            )
            copy.start()
            copies.append(copy)
        window[pl.ds(pl.multiple_of(REACH * BLOCK + mine, PIECE), PIECE), :] = piece[pl.ds(mine, PIECE), :]

    lane = iota((1, WIDTH), 1)
    start = jnp.int32(0)
    starts = jnp.full((1, WIDTH), 1 << 30, jnp.int32)
    ends = jnp.full((1, WIDTH), 1 << 30, jnp.int32)
    for doc in range(NDOCS):
        end = start + lens_ref[doc]
        starts = jnp.where(lane == doc, start, starts)
        ends = jnp.where(lane == doc, end, ends)
        start = end
    starts = jnp.where(lane == NDOCS, -(1 << 30), starts)
    ends = jnp.where(lane == NDOCS, 0, ends)

    key_pos = (c - REACH) * BLOCK + iota((WINDOW, WIDTH), 0)
    kaug[...] = jnp.where((starts <= key_pos) & (key_pos < ends), 1.0, 0.0).astype(BF16)
    row_pos = c * BLOCK + iota((ROWS, WIDTH), 0) // HEADS
    outside = jnp.where((starts <= row_pos) & (row_pos < ends), 0.0, -FAR)
    qaug[...] = jnp.where(iota((ROWS, WIDTH), 1) <= NDOCS, outside, 0.0).astype(BF16)

    for t in range(TILES):
        g_t = jnp.transpose(g_ref[pl.ds(TILE * t, TILE), :])
        o_t = jnp.transpose(o_ref[pl.ds(TILE * t, TILE), :])
        gt[t] = g_t
        delta[pl.ds(t, 1), :] = jnp.sum(
            g_t.astype(F32) * o_t.astype(F32), axis=0, keepdims=True
        )
    dka[...] = jnp.zeros_like(dka)
    dva[...] = jnp.zeros_like(dva)

    def cross(window, i, hop):
        at = REACH * BLOCK - 2 * BLOCK * hop
        return pltpu.make_async_remote_copy(
            src_ref=window.at[pl.ds(at, BLOCK)],
            dst_ref=window.at[pl.ds(at - 2 * BLOCK, BLOCK)],
            send_sem=cs_sem.at[i, hop],
            recv_sem=cr_sem.at[i, hop],
            device_id={"ctx": nxt},
            device_id_type=MESH,
        )

    def aside(window, i, hop):
        at = (REACH - 2 * hop) * BLOCK - 2 * BLOCK * core
        return pltpu.make_async_remote_copy(
            src_ref=window.at[pl.ds(pl.multiple_of(at, BLOCK), BLOCK)],
            dst_ref=window.at[pl.ds((REACH - 2 * hop - 1) * BLOCK, BLOCK)],
            send_sem=cs_sem.at[i, 2 + hop],
            recv_sem=cr_sem.at[i, 2 + hop],
            device_id={"ctx": sib},
            device_id_type=MESH,
        )

    cross_k = [cross(kb, 0, hop) for hop in range(2)]
    cross_v = [cross(vb, 1, hop) for hop in range(2)]
    aside_k = [aside(kb, 0, hop) for hop in range(2)]
    aside_v = [aside(vb, 1, hop) for hop in range(2)]

    for copies, crossing, siding in ((k_copies, cross_k, aside_k), (v_copies, cross_v, aside_v)):
        for copy in copies:
            copy.wait_recv()
        crossing[0].start()

        @pl.when(core == 0)
        def _(siding=siding):
            siding[0].start()

    def relay(crossing, siding):
        crossing[0].wait_recv()
        crossing[1].start()

        @pl.when(core == 0)
        def _():
            siding[1].start()

        @pl.when(core == 1)
        def _():
            siding[0].start()

    def relay_last(crossing, siding):
        crossing[1].wait_recv()

        @pl.when(core == 1)
        def _():
            siding[1].start()

    def scores(b):
        off, rows = CHUNKS[b]

        def tile(t, carry):
            at = pl.ds(pl.multiple_of(STEP * t + off, STEP), rows)
            here = pl.ds(pl.multiple_of(TILE * t, TILE), TILE)
            left = jnp.concatenate([kb[at, :], kaug[at, :]], axis=1)
            right = jnp.concatenate([q_ref[here, :], qaug[here, :]], axis=1)
            s = dot(left, right, NT)
            if rows > BLOCK:
                own = jnp.where(
                    iota((STEP, TILE), 0) <= iota((STEP, TILE), 1) // HEADS, s[BLOCK:], -1e30
                )
                s = jnp.concatenate([s[:BLOCK], own], axis=0)
            m = jnp.max(s, axis=0, keepdims=True)
            e = jnp.exp2((s - m) * RATE)
            m_st[b, pl.ds(t, 1), :] = m
            l_st[b, pl.ds(t, 1), :] = jnp.sum(e, axis=0, keepdims=True)
            band[t, pl.ds(off, rows), :] = e.astype(BF16)
            return carry

        lax.fori_loop(0, TILES, tile, 0, unroll=2)

    relay(cross_k, aside_k)
    aside_k[0].wait_recv()
    scores(3)
    relay(cross_v, aside_v)
    scores(2)
    relay_last(cross_k, aside_k)
    aside_k[1].wait_recv()
    scores(1)
    relay_last(cross_v, aside_v)
    scores(0)

    top = jnp.maximum(jnp.maximum(m_st[0], m_st[1]), jnp.maximum(m_st[2], m_st[3]))
    parts = [jnp.exp2((m_st[b] - top) * RATE) for b in range(4)]
    total = sum(part * l_st[b] for b, part in enumerate(parts))
    for b, part in enumerate(parts):
        share = part / total
        w_st[b] = share
        wd_st[b] = share * delta[...]

    def grads(b):
        off, rows = CHUNKS[b]

        def tile(t, carry):
            at = pl.ds(pl.multiple_of(STEP * t + off, STEP), rows)
            here = pl.ds(pl.multiple_of(TILE * t, TILE), TILE)
            g_t = (gt[t].astype(F32) * w_st[b, pl.ds(t, 1), :]).astype(BF16)
            dp = dot(vb[at, :], g_t)
            e = band[t, pl.ds(off, rows), :]
            ds = e * (dp - wd_st[b, pl.ds(t, 1), :]).astype(BF16)
            band[t, pl.ds(off, rows), :] = ds
            dva[at, :] += dot(e, g_t, NT)
            dka[at, :] += dot(ds, q_ref[here, :])
            return carry

        lax.fori_loop(0, TILES, tile, 0, unroll=2)

    def back(i, hop, other):
        return pltpu.make_async_remote_copy(
            src_ref=stage.at[i, hop],
            dst_ref=got.at[i, hop],
            send_sem=rs_sem.at[i, hop],
            recv_sem=rr_sem.at[i, hop],
            device_id={"ctx": other},
            device_id_type=MESH,
        )

    accs = (dva, dka)
    side_b = [back(i, 0, sib) for i in range(2)]
    side_a = [back(i, 1, sib) for i in range(2)]
    far_b = [back(i, 2, prv) for i in range(2)]
    far_a = [back(i, 3, prv) for i in range(2)]

    def slot(s):
        return pl.ds(BLOCK * s, BLOCK)

    def hand(copy, i, hop, value):
        stage[i, hop] = value.astype(BF16)
        copy.start()

    aside_v[1].wait_recv()
    grads(0)
    for i in range(2):

        @pl.when(core == 0)
        def _(i=i):
            hand(far_b[i], i, 2, accs[i][slot(0), :])

    grads(1)
    for i in range(2):
        hand(side_b[i], i, 0, accs[i][slot(1), :])
    aside_v[0].wait_recv()
    grads(2)
    for i in range(2):
        side_b[i].wait_recv()

        @pl.when(core == 1)
        def _(i=i):
            hand(far_b[i], i, 2, accs[i][slot(0), :] + got[i, 0].astype(F32))

    grads(3)
    for i in range(2):
        hand(side_a[i], i, 1, accs[i][slot(3), :])
    for i in range(2):
        far_b[i].wait_recv()

        @pl.when(core == 0)
        def _(i=i):
            hand(far_a[i], i, 3, accs[i][slot(2), :] + got[i, 0].astype(F32) + got[i, 2].astype(F32))

    for i in range(2):
        side_a[i].wait_recv()

        @pl.when(core == 1)
        def _(i=i):
            hand(far_a[i], i, 3, accs[i][slot(2), :] + got[i, 1].astype(F32) + got[i, 2].astype(F32))

    def queries(t, carry):
        at = pl.ds(pl.multiple_of(STEP * t, STEP), BAND)
        here = pl.ds(pl.multiple_of(TILE * t, TILE), TILE)
        dq_ref[here, :] = (dot(band[t], kb[at, :], TN) * SCALE).astype(BF16)
        return carry

    lax.fori_loop(0, TILES, queries, 0)

    last = []
    for i in range(2):
        far_a[i].wait_recv()
        whole = accs[i][slot(4), :] + got[i, 3].astype(F32)
        whole = whole + jnp.where(core == 0, got[i, 1].astype(F32), 0.0)
        if i == 1:
            whole = whole * SCALE
        sent[i] = whole.astype(BF16)
        for o, peer in enumerate(peers):
            copy = pltpu.make_async_remote_copy(
                src_ref=sent.at[i, pl.ds(pl.multiple_of(PIECE * peer, PIECE), PIECE)],
                dst_ref=fin.at[i, pl.ds(mine, PIECE)],
                send_sem=fs_sem.at[i, o],
                recv_sem=fr_sem.at[i, o],
                device_id={"head": peer},
                device_id_type=MESH,
            )
            copy.start()
            last.append(copy)
        fin[i, pl.ds(mine, PIECE), :] = sent[i, pl.ds(mine, PIECE), :]

    place = jnp.where(
        row == (col % PIECE) * GROUPS + col // PIECE, 1.0, 0.0
    ).astype(BF16)
    for i, out_ref in enumerate((dv_ref, dk_ref)):
        for copy in last[i * (GROUPS - 1) : (i + 1) * (GROUPS - 1)]:
            copy.wait_recv()
        out_ref[...] = dot(place, fin[i]).astype(BF16)

    for copy in k_copies + v_copies + last:
        copy.wait_send()
    for group in (cross_k, cross_v, aside_k, aside_v, side_a, side_b, far_a, far_b):
        for copy in group:
            copy.wait_send()


def solution(mesh):
    n_ctx = mesh.shape["ctx"]
    dma = pltpu.SemaphoreType.DMA

    def body(queries, keys, values, output, grad_output, doc_lengths):
        flat = lambda x: x.reshape(-1, WIDTH)
        vmem = pl.BlockSpec(memory_space=pltpu.VMEM)
        piece = PIECE * GROUPS
        dq, dk, dv = pl.pallas_call(
            functools.partial(kernel, n_ctx),
            out_shape=(
                jax.ShapeDtypeStruct((ROWS, WIDTH), BF16),
                jax.ShapeDtypeStruct((piece, WIDTH), BF16),
                jax.ShapeDtypeStruct((piece, WIDTH), BF16),
            ),
            in_specs=[pl.BlockSpec(memory_space=pltpu.SMEM)] + [vmem] * 5,
            out_specs=(vmem, vmem, vmem),
            scratch_shapes=[
                pltpu.VMEM((WINDOW, WIDTH), BF16),
                pltpu.VMEM((WINDOW, WIDTH), BF16),
                pltpu.VMEM((piece, WIDTH), BF16),
                pltpu.VMEM((piece, WIDTH), BF16),
                pltpu.VMEM((WINDOW, WIDTH), BF16),
                pltpu.VMEM((ROWS, WIDTH), BF16),
                pltpu.VMEM((TILES, WIDTH, TILE), BF16),
                pltpu.VMEM((TILES, TILE), F32),
                pltpu.VMEM((TILES, BAND, TILE), BF16),
                pltpu.VMEM((4, TILES, TILE), F32),
                pltpu.VMEM((4, TILES, TILE), F32),
                pltpu.VMEM((4, TILES, TILE), F32),
                pltpu.VMEM((4, TILES, TILE), F32),
                pltpu.VMEM((WINDOW, WIDTH), F32),
                pltpu.VMEM((WINDOW, WIDTH), F32),
                pltpu.VMEM((2, 4, BLOCK, WIDTH), BF16),
                pltpu.VMEM((2, 4, BLOCK, WIDTH), BF16),
                pltpu.VMEM((2, BLOCK, WIDTH), BF16),
                pltpu.VMEM((2, BLOCK, WIDTH), BF16),
                dma((GROUPS - 1,)),
                dma((GROUPS - 1,)),
                dma((GROUPS - 1,)),
                dma((GROUPS - 1,)),
                dma((2, 4)),
                dma((2, 4)),
                dma((2, 4)),
                dma((2, 4)),
                dma((2, GROUPS - 1)),
                dma((2, GROUPS - 1)),
            ],
            compiler_params=pltpu.CompilerParams(
                collective_id=0, has_side_effects=True, vmem_limit_bytes=48 << 20
            ),
        )(doc_lengths, flat(queries), flat(output), flat(grad_output), flat(keys), flat(values))
        return (
            dq.reshape(queries.shape),
            dk.reshape(keys.shape),
            dv.reshape(values.shape),
        )

    return jax.shard_map(
        body,
        mesh=mesh,
        in_specs=(
            P("ctx", "head", None),
            P(("ctx", "head"), None, None),
            P(("ctx", "head"), None, None),
            P("ctx", "head", None),
            P("ctx", "head", None),
            P(),
        ),
        out_specs=(
            P("ctx", "head", None),
            P(("ctx", "head"), None, None),
            P(("ctx", "head"), None, None),
        ),
        check_vma=False,
    )
```

```python
import functools
import math

import jax
import jax.numpy as jnp
from jax import lax
from jax.experimental import pallas as pl
from jax.experimental.pallas import tpu as pltpu
from jax.sharding import PartitionSpec as P

MESH = pl.DeviceIdType.MESH
F32 = jnp.float32
BF16 = jnp.bfloat16

BLOCK = 256
REACH = 4
WINDOW = (REACH + 1) * BLOCK
WIDTH = 128
HEADS = 8
GROUPS = 8
ROWS = BLOCK * HEADS
TILE = 256
TILES = ROWS // TILE
STEP = TILE // HEADS
PIECE = BLOCK // GROUPS
NDOCS = 16
FAR = 2.0**20
SCALE = 1.0 / math.sqrt(WIDTH)
RATE = SCALE / math.log(2.0)

HALF = BLOCK // 2


def reach(s, t):
    if s == REACH:
        return (0, HALF) if t < TILES // 2 else (0, BLOCK)
    if s == 0 and t >= TILES // 2:
        return (HALF, BLOCK)
    return (0, BLOCK)


def halves(s):
    if s == REACH:
        return ((0, HALF, 0, ROWS), (HALF, BLOCK, ROWS // 2, ROWS))
    if s == 0:
        return ((0, HALF, 0, ROWS // 2), (HALF, BLOCK, 0, ROWS))
    return ((0, BLOCK, 0, ROWS),)


VMEM = (64 << 20) - (640 << 10)

NT = (((1,), (1,)), ((), ()))
NN = (((1,), (0,)), ((), ()))
TN = (((0,), (0,)), ((), ()))


def dot(a, b, dims=NN):
    return lax.dot_general(a, b, dims, preferred_element_type=F32)


def iota(shape, dim):
    return lax.broadcasted_iota(jnp.int32, shape, dim)


def kernel(
    n_ctx,
    lens_any, q_any, o_any, g_any, k_any, v_any,
    dq_any, fin_any,
    dq_ref, lens_ref, q_ref, o_ref, g_ref, k_ref, v_ref,
    kb, vb, order, kp, vp, kaug, qaug, gt, delta, band, m_st, l_st, w_st, wd_st,
    gw, dka, dva, stage, got, sent,
    in_sem, out_sem, ks_sem, kr_sem, vs_sem, vr_sem, cs_sem, cr_sem, rs_sem, rr_sem, fs_sem, fr_sem,
):
    c = lax.axis_index("ctx")
    z = lax.axis_index("head")
    core = lax.rem(c, 2)
    sib = c + 1 - 2 * core
    ahead = {o: lax.rem(c + o, n_ctx) for o in (1, 2, 4)}
    behind = {o: lax.rem(c + n_ctx - o, n_ctx) for o in (1, 2, 4)}
    peers = [lax.rem(z + o, GROUPS) for o in range(1, GROUPS)]

    barrier = pltpu.get_barrier_semaphore()
    for peer in peers:
        pl.semaphore_signal(barrier, inc=1, device_id={"head": peer}, device_id_type=MESH)
    for other in (*ahead.values(), *behind.values()):
        pl.semaphore_signal(barrier, inc=1, device_id={"ctx": other}, device_id_type=MESH)

    loads = []
    for i, (source, target) in enumerate(
        (
            (k_any, k_ref), (v_any, v_ref), (lens_any, lens_ref),
            (q_any, q_ref), (g_any, g_ref), (o_any, o_ref),
        )
    ):
        load = pltpu.make_async_copy(source, target, in_sem.at[i])
        load.start()
        loads.append(load)
    row, col = iota((BLOCK, BLOCK), 0), iota((BLOCK, BLOCK), 1)
    order[...] = jnp.where(
        col == (row % PIECE) * GROUPS + row // PIECE, 1.0, 0.0
    ).astype(BF16)
    mine = pl.multiple_of(PIECE * z, PIECE)
    k_copies, v_copies = [], []
    for i, (given, piece, window, send, recv, copies) in enumerate(
        (
            (k_ref, kp, kb, ks_sem, kr_sem, k_copies),
            (v_ref, vp, vb, vs_sem, vr_sem, v_copies),
        )
    ):
        loads[i].wait()
        piece[...] = dot(order[...], given[...]).astype(BF16)
        if i == 0:
            pl.semaphore_wait(barrier, GROUPS - 1 + len(ahead) + len(behind))
        for o, peer in enumerate(peers):
            copy = pltpu.make_async_remote_copy(
                src_ref=piece.at[pl.ds(pl.multiple_of(PIECE * peer, PIECE), PIECE)],
                dst_ref=window.at[pl.ds(pl.multiple_of(REACH * BLOCK + mine, PIECE), PIECE)],
                send_sem=send.at[o],
                recv_sem=recv.at[o],
                device_id={"head": peer},
                device_id_type=MESH,
            )
            copy.start()
            copies.append(copy)
        window[pl.ds(pl.multiple_of(REACH * BLOCK + mine, PIECE), PIECE), :] = piece[pl.ds(mine, PIECE), :]

    for load in loads[2:]:
        load.wait()
    lane = iota((1, WIDTH), 1)
    start = jnp.int32(0)
    starts = jnp.full((1, WIDTH), 1 << 30, jnp.int32)
    ends = jnp.full((1, WIDTH), 1 << 30, jnp.int32)
    for doc in range(NDOCS):
        end = start + lens_ref[doc]
        starts = jnp.where(lane == doc, start, starts)
        ends = jnp.where(lane == doc, end, ends)
        start = end
    starts = jnp.where(lane == NDOCS, -(1 << 30), starts)
    ends = jnp.where(lane == NDOCS, 0, ends)

    key_pos = (c - REACH) * BLOCK + iota((WINDOW, WIDTH), 0)
    kaug[...] = jnp.where((starts <= key_pos) & (key_pos < ends), 1.0, 0.0).astype(BF16)
    row_pos = c * BLOCK + lax.shift_right_logical(iota((ROWS, WIDTH), 0), 3)
    outside = jnp.where((starts <= row_pos) & (row_pos < ends), 0.0, -FAR)
    qaug[...] = jnp.where(iota((ROWS, WIDTH), 1) <= NDOCS, outside, 0.0).astype(BF16)

    for t in range(TILES):
        g_t = jnp.transpose(g_ref[pl.ds(TILE * t, TILE), :])
        o_t = jnp.transpose(o_ref[pl.ds(TILE * t, TILE), :])
        gt[:, pl.ds(TILE * t, TILE)] = g_t
        delta[pl.ds(t, 1), :] = jnp.sum(
            g_t.astype(F32) * o_t.astype(F32), axis=0, keepdims=True
        )

    def ahead_by(window, i, o, other):
        return pltpu.make_async_remote_copy(
            src_ref=window.at[pl.ds(REACH * BLOCK, BLOCK)],
            dst_ref=window.at[pl.ds((REACH - o) * BLOCK, BLOCK)],
            send_sem=cs_sem.at[i, o // 2],
            recv_sem=cr_sem.at[i, o // 2],
            device_id={"ctx": other},
            device_id_type=MESH,
        )

    def aside(window, i, hop):
        at = (REACH - 2 * hop) * BLOCK - 2 * BLOCK * core
        return pltpu.make_async_remote_copy(
            src_ref=window.at[pl.ds(pl.multiple_of(at, BLOCK), BLOCK)],
            dst_ref=window.at[pl.ds((REACH - 2 * hop - 1) * BLOCK, BLOCK)],
            send_sem=cs_sem.at[i, 3 * hop],
            recv_sem=cr_sem.at[i, 3 * hop],
            device_id={"ctx": sib},
            device_id_type=MESH,
        )

    k_ahead = {o: ahead_by(kb, 0, o, ahead[o]) for o in (1, 2, 4)}
    v_ahead = {o: ahead_by(vb, 1, o, ahead[o]) for o in (2, 4)}
    k_side = aside(kb, 0, 1)
    v_side = [aside(vb, 1, hop) for hop in range(2)]

    def scores(s):
        for t in range(TILES):
            lo, hi = reach(s, t)
            at = pl.ds(BLOCK * s + lo, hi - lo)
            here = pl.ds(TILE * t, TILE)
            left = jnp.concatenate([kb[at, :], kaug[at, :]], axis=1)
            right = jnp.concatenate([q_ref[here, :], qaug[here, :]], axis=1)
            x = dot(left, right, NT)
            if s == REACH:
                key = hi - HALF + iota((HALF, TILE), 0)
                query = STEP * t + lax.shift_right_logical(iota((HALF, TILE), 1), 3)
                own = jnp.where(key <= query, x[hi - HALF :], -1e30)
                x = own if hi == HALF else jnp.concatenate([x[:HALF], own], axis=0)
            m = jnp.max(x, axis=0, keepdims=True)
            e = jnp.exp2((x - m) * RATE)
            m_st[s, pl.ds(t, 1), :] = m
            l_st[s, pl.ds(t, 1), :] = jnp.sum(e, axis=0, keepdims=True)
            band[at, here] = e.astype(BF16)

    for copy in k_copies:
        copy.wait_recv()
    for o in (1, 2, 4):
        k_ahead[o].start()
    for copy in v_copies:
        copy.wait_recv()

    @pl.when(core == 0)
    def _():
        v_side[0].start()

    scores(4)
    k_ahead[1].wait_recv()
    scores(3)
    k_ahead[2].wait_recv()

    @pl.when(core == 0)
    def _():
        k_side.start()

    k_ahead[4].wait_recv()

    @pl.when(core == 1)
    def _():
        k_side.start()

    for o in (2, 4):
        v_ahead[o].start()
    scores(2)
    scores(0)
    k_side.wait_recv()
    scores(1)

    slots = range(REACH + 1)
    top = functools.reduce(jnp.maximum, [m_st[s] for s in slots])
    parts = [jnp.exp2((m_st[s] - top) * RATE) for s in slots]
    total = sum(part * l_st[s] for s, part in enumerate(parts))
    for s, part in enumerate(parts):
        share = part / total
        w_st[s] = share
        wd_st[s] = share * delta[...]

    def value_grads(s):
        for t in range(TILES):
            here = pl.ds(TILE * t, TILE)
            gw[s, :, here] = (gt[:, here].astype(F32) * w_st[s, pl.ds(t, 1), :]).astype(BF16)
        for lo, hi, first, end in halves(s):
            at, rows = pl.ds(BLOCK * s + lo, hi - lo), pl.ds(first, end - first)
            dva[at, :] = dot(band[at, rows], gw[s, :, rows], NT)

    def key_grads(s):
        for t in range(TILES):
            lo, hi = reach(s, t)
            at = pl.ds(BLOCK * s + lo, hi - lo)
            here = pl.ds(TILE * t, TILE)
            dp = dot(vb[at, :], gw[s, :, here])
            band[at, here] = band[at, here] * (dp - wd_st[s, pl.ds(t, 1), :]).astype(BF16)
        for lo, hi, first, end in halves(s):
            at, rows = pl.ds(BLOCK * s + lo, hi - lo), pl.ds(first, end - first)
            dka[at, :] = dot(band[at, rows], q_ref[rows, :])

    def back(i, hop, other):
        return pltpu.make_async_remote_copy(
            src_ref=stage.at[i, hop],
            dst_ref=got.at[i, hop],
            send_sem=rs_sem.at[i, hop],
            recv_sem=rr_sem.at[i, hop],
            device_id={"ctx": other},
            device_id_type=MESH,
        )

    accs = (dva, dka)
    returns = [
        [back(i, hop, other) for hop, other in enumerate((sib, behind[1], behind[2], behind[4]))]
        for i in range(2)
    ]

    def hand(i, hop, s, extra):
        value = accs[i][pl.ds(BLOCK * s, BLOCK), :]
        if extra:
            value = value + got[i, 0].astype(F32)
        stage[i, hop] = value.astype(BF16)
        returns[i][hop].start()

    def grads(i, part, between=((), ())):
        part(0)

        @pl.when(core == 0)
        def _():
            hand(i, 3, 0, False)

        for step in between[0]:
            step()
        part(1)
        hand(i, 0, 1, False)
        for step in between[1]:
            step()
        part(2)

        @pl.when(core == 1)
        def _():
            hand(i, 2, 2, False)

        part(3)
        hand(i, 1, 3, False)
        returns[i][0].wait_recv()

        @pl.when(core == 0)
        def _():
            hand(i, 2, 2, True)

        @pl.when(core == 1)
        def _():
            hand(i, 3, 0, True)

        part(4)

    def relay_near():
        v_ahead[2].wait_recv()

        @pl.when(core == 0)
        def _():
            v_side[1].start()

        @pl.when(core == 1)
        def _():
            v_side[0].start()

    def relay_far():
        v_ahead[4].wait_recv()

        @pl.when(core == 1)
        def _():
            v_side[1].start()

    last = []

    def finish(i):
        for hop in (3, 2, 1):
            returns[i][hop].wait_recv()
        whole = accs[i][pl.ds(REACH * BLOCK, BLOCK), :]
        for hop in (1, 2, 3):
            whole = whole + got[i, hop].astype(F32)
        if i == 1:
            whole = whole * SCALE
        sent[i] = whole.astype(BF16)
        for o, peer in enumerate(peers):
            copy = pltpu.make_async_remote_copy(
                src_ref=sent.at[i, pl.ds(pl.multiple_of(PIECE * peer, PIECE), PIECE)],
                dst_ref=fin_any.at[i, pl.ds(mine, PIECE)],
                send_sem=fs_sem.at[i, o],
                recv_sem=fr_sem.at[i, o],
                device_id={"head": peer},
                device_id_type=MESH,
            )
            copy.start()
            last.append(copy)
        save = pltpu.make_async_copy(
            sent.at[i, pl.ds(mine, PIECE)], fin_any.at[i, pl.ds(mine, PIECE)], out_sem.at[i]
        )
        save.start()
        saves.append(save)

    saves = []
    grads(0, value_grads, ((relay_near,), (relay_far,)))
    for copy in v_side:
        copy.wait_recv()
    grads(1, key_grads)
    finish(0)

    for t in range(TILES):
        here = pl.ds(TILE * t, TILE)
        first, end = reach(0, t)[0], REACH * BLOCK + reach(REACH, t)[1]
        at = pl.ds(first, end - first)
        dq_ref[here, :] = (dot(band[at, here], kb[at, :], TN) * SCALE).astype(BF16)

    save = pltpu.make_async_copy(dq_ref, dq_any, out_sem.at[2])
    save.start()
    saves.append(save)
    finish(1)

    for copy in last:
        copy.wait_recv()
    for copy in (*k_copies, *v_copies, *k_ahead.values(), *v_ahead.values(), k_side, *v_side):
        copy.wait_send()
    for copy in (*returns[0], *returns[1], *last):
        copy.wait_send()
    for save in saves:
        save.wait()


PARTS = 4


def store(dq_any, fin_any, dq_out, dk_out, dv_out, dq_ref, fin, dk_ref, dv_ref, load_sem, save_sem):
    part = [pl.ds(ROWS // PARTS * i, ROWS // PARTS) for i in range(PARTS)]
    loads = [pltpu.make_async_copy(fin_any, fin, load_sem.at[PARTS])] + [
        pltpu.make_async_copy(dq_any.at[p], dq_ref.at[p], load_sem.at[i]) for i, p in enumerate(part)
    ]
    for load in loads:
        load.start()
    row, col = iota((BLOCK, BLOCK), 0), iota((BLOCK, BLOCK), 1)
    place = jnp.where(
        row == (col % PIECE) * GROUPS + col // PIECE, 1.0, 0.0
    ).astype(BF16)
    saves = []

    def save(source, target):
        copy = pltpu.make_async_copy(source, target, save_sem.at[len(saves)])
        copy.start()
        saves.append(copy)

    loads[0].wait()
    for i, (ref, out) in enumerate(((dv_ref, dv_out), (dk_ref, dk_out))):
        ref[...] = dot(place, fin[i]).astype(BF16)
        save(ref, out)
    for load, p in zip(loads[1:], part):
        load.wait()
        save(dq_ref.at[p], dq_out.at[p])
    for copy in saves:
        copy.wait()


def solution(mesh):
    n_ctx = mesh.shape["ctx"]
    dma = pltpu.SemaphoreType.DMA

    def body(queries, keys, values, output, grad_output, doc_lengths):
        flat = lambda x: x.reshape(-1, WIDTH)
        piece = PIECE * GROUPS
        dq, fin = pl.pallas_call(
            functools.partial(kernel, n_ctx),
            out_shape=(
                jax.ShapeDtypeStruct((ROWS, WIDTH), BF16),
                jax.ShapeDtypeStruct((2, piece, WIDTH), BF16),
            ),
            in_specs=[pl.BlockSpec(memory_space=pl.ANY)] * 6,
            out_specs=[pl.BlockSpec(memory_space=pl.ANY)] * 2,
            scratch_shapes=[
                pltpu.VMEM((ROWS, WIDTH), BF16),
                pltpu.SMEM((NDOCS,), jnp.int32),
                pltpu.VMEM((ROWS, WIDTH), BF16),
                pltpu.VMEM((ROWS, WIDTH), BF16),
                pltpu.VMEM((ROWS, WIDTH), BF16),
                pltpu.VMEM((piece, WIDTH), BF16),
                pltpu.VMEM((piece, WIDTH), BF16),
                pltpu.VMEM((WINDOW, WIDTH), BF16),
                pltpu.VMEM((WINDOW, WIDTH), BF16),
                pltpu.VMEM((BLOCK, BLOCK), BF16),
                pltpu.VMEM((piece, WIDTH), BF16),
                pltpu.VMEM((piece, WIDTH), BF16),
                pltpu.VMEM((WINDOW, WIDTH), BF16),
                pltpu.VMEM((ROWS, WIDTH), BF16),
                pltpu.VMEM((WIDTH, ROWS), BF16),
                pltpu.VMEM((TILES, TILE), F32),
                pltpu.VMEM((WINDOW, ROWS), BF16),
                pltpu.VMEM((REACH + 1, TILES, TILE), F32),
                pltpu.VMEM((REACH + 1, TILES, TILE), F32),
                pltpu.VMEM((REACH + 1, TILES, TILE), F32),
                pltpu.VMEM((REACH + 1, TILES, TILE), F32),
                pltpu.VMEM((REACH + 1, WIDTH, ROWS), BF16),
                pltpu.VMEM((WINDOW, WIDTH), F32),
                pltpu.VMEM((WINDOW, WIDTH), F32),
                pltpu.VMEM((2, 4, BLOCK, WIDTH), BF16),
                pltpu.VMEM((2, 4, BLOCK, WIDTH), BF16),
                pltpu.VMEM((2, BLOCK, WIDTH), BF16),
                dma((6,)),
                dma((3,)),
                dma((GROUPS - 1,)),
                dma((GROUPS - 1,)),
                dma((GROUPS - 1,)),
                dma((GROUPS - 1,)),
                dma((2, 4)),
                dma((2, 4)),
                dma((2, 4)),
                dma((2, 4)),
                dma((2, GROUPS - 1)),
                dma((2, GROUPS - 1)),
            ],
            compiler_params=pltpu.CompilerParams(
                collective_id=0, has_side_effects=True, vmem_limit_bytes=VMEM
            ),
        )(doc_lengths, flat(queries), flat(output), flat(grad_output), flat(keys), flat(values))
        dq, dk, dv = pl.pallas_call(
            store,
            out_shape=(
                jax.ShapeDtypeStruct((ROWS, WIDTH), BF16),
                jax.ShapeDtypeStruct((piece, WIDTH), BF16),
                jax.ShapeDtypeStruct((piece, WIDTH), BF16),
            ),
            in_specs=[pl.BlockSpec(memory_space=pl.ANY)] * 2,
            out_specs=[pl.BlockSpec(memory_space=pl.ANY)] * 3,
            scratch_shapes=[
                pltpu.VMEM((ROWS, WIDTH), BF16),
                pltpu.VMEM((2, piece, WIDTH), BF16),
                pltpu.VMEM((piece, WIDTH), BF16),
                pltpu.VMEM((piece, WIDTH), BF16),
                dma((PARTS + 1,)),
                dma((PARTS + 2,)),
            ],
            compiler_params=pltpu.CompilerParams(vmem_limit_bytes=VMEM),
        )(dq, fin)
        return (
            dq.reshape(queries.shape),
            dk.reshape(keys.shape),
            dv.reshape(values.shape),
        )

    return jax.shard_map(
        body,
        mesh=mesh,
        in_specs=(
            P("ctx", "head", None),
            P(("ctx", "head"), None, None),
            P(("ctx", "head"), None, None),
            P("ctx", "head", None),
            P("ctx", "head", None),
            P(),
        ),
        out_specs=(
            P("ctx", "head", None),
            P(("ctx", "head"), None, None),
            P(("ctx", "head"), None, None),
        ),
        check_vma=False,
    )
```

```python
import functools
import math

import jax
import jax.numpy as jnp
from jax import lax
from jax.experimental import pallas as pl
from jax.experimental.pallas import tpu as pltpu
from jax.sharding import PartitionSpec as P

MESH = pl.DeviceIdType.MESH
F32 = jnp.float32
BF16 = jnp.bfloat16

BLOCK = 256
REACH = 4
WINDOW = (REACH + 1) * BLOCK
WIDTH = 128
HEADS = 8
GROUPS = 8
ROWS = BLOCK * HEADS
TILE = 256
TILES = ROWS // TILE
STEP = TILE // HEADS
PIECE = BLOCK // GROUPS
NDOCS = 16
FAR = 2.0**20
SCALE = 1.0 / math.sqrt(WIDTH)
RATE = SCALE / math.log(2.0)

HALF = BLOCK // 2


def reach(s, t):
    if s == REACH:
        return (0, HALF) if t < TILES // 2 else (0, BLOCK)
    if s == 0 and t >= TILES // 2:
        return (HALF, BLOCK)
    return (0, BLOCK)


def halves(s):
    if s == REACH:
        return ((0, HALF, 0, ROWS), (HALF, BLOCK, ROWS // 2, ROWS))
    if s == 0:
        return ((0, HALF, 0, ROWS // 2), (HALF, BLOCK, 0, ROWS))
    return ((0, BLOCK, 0, ROWS),)


VMEM = (64 << 20) - (640 << 10)

NT = (((1,), (1,)), ((), ()))
NN = (((1,), (0,)), ((), ()))
TN = (((0,), (0,)), ((), ()))


def dot(a, b, dims=NN):
    return lax.dot_general(a, b, dims, preferred_element_type=F32)


def iota(shape, dim):
    return lax.broadcasted_iota(jnp.int32, shape, dim)


def kernel(
    n_ctx,
    lens_any, q_any, o_any, g_any, k_any, v_any,
    dq_any, fin_any,
    dq_ref, lens_ref, q_ref, o_ref, g_ref, k_ref, v_ref,
    kb, vb, order, kp, vp, kaug, qaug, gt, delta, band, m_st, l_st, w_st, wd_st,
    gw, dka, dva, stage, got, sent,
    in_sem, out_sem, ks_sem, kr_sem, vs_sem, vr_sem, cs_sem, cr_sem, rs_sem, rr_sem, fs_sem, fr_sem,
):
    c = lax.axis_index("ctx")
    z = lax.axis_index("head")
    core = lax.rem(c, 2)
    sib = c + 1 - 2 * core
    ahead = {o: lax.rem(c + o, n_ctx) for o in (1, 2, 4)}
    behind = {o: lax.rem(c + n_ctx - o, n_ctx) for o in (1, 2, 4)}
    peers = [lax.rem(z + o, GROUPS) for o in (4, 3, 5, 2, 6, 1, 7)]

    loads = []
    for i, (source, target) in enumerate(
        (
            (k_any, k_ref), (v_any, v_ref), (lens_any, lens_ref),
            (q_any, q_ref), (g_any, g_ref), (o_any, o_ref),
        )
    ):
        load = pltpu.make_async_copy(source, target, in_sem.at[i])
        loads.append(load)
    loads[0].start()
    loads[1].start()
    barrier = pltpu.get_barrier_semaphore()
    for peer in peers:
        pl.semaphore_signal(barrier, inc=1, device_id={"head": peer}, device_id_type=MESH)
    for other in (*ahead.values(), *behind.values()):
        pl.semaphore_signal(barrier, inc=1, device_id={"ctx": other}, device_id_type=MESH)

    for load in loads[2:]:
        load.start()
    row, col = iota((BLOCK, BLOCK), 0), iota((BLOCK, BLOCK), 1)
    order[...] = jnp.where(
        col == (row % PIECE) * GROUPS + row // PIECE, 1.0, 0.0
    ).astype(BF16)
    mine = pl.multiple_of(PIECE * z, PIECE)
    k_copies, v_copies = [], []
    for i, (given, piece, window, send, recv, copies) in enumerate(
        (
            (k_ref, kp, kb, ks_sem, kr_sem, k_copies),
            (v_ref, vp, vb, vs_sem, vr_sem, v_copies),
        )
    ):
        loads[i].wait()
        piece[...] = dot(order[...], given[...]).astype(BF16)
        if i == 0:
            pl.semaphore_wait(barrier, GROUPS - 1 + len(ahead) + len(behind))
        for o, peer in enumerate(peers):
            copy = pltpu.make_async_remote_copy(
                src_ref=piece.at[pl.ds(pl.multiple_of(PIECE * peer, PIECE), PIECE)],
                dst_ref=window.at[pl.ds(pl.multiple_of(REACH * BLOCK + mine, PIECE), PIECE)],
                send_sem=send.at[o],
                recv_sem=recv.at[o],
                device_id={"head": peer},
                device_id_type=MESH,
            )
            copy.start()
            copies.append(copy)
        window[pl.ds(pl.multiple_of(REACH * BLOCK + mine, PIECE), PIECE), :] = piece[pl.ds(mine, PIECE), :]

    for load in loads[2:]:
        load.wait()
    lane = iota((1, WIDTH), 1)
    start = jnp.int32(0)
    starts = jnp.full((1, WIDTH), 1 << 30, jnp.int32)
    ends = jnp.full((1, WIDTH), 1 << 30, jnp.int32)
    for doc in range(NDOCS):
        end = start + lens_ref[doc]
        starts = jnp.where(lane == doc, start, starts)
        ends = jnp.where(lane == doc, end, ends)
        start = end
    starts = jnp.where(lane == NDOCS, -(1 << 30), starts)
    ends = jnp.where(lane == NDOCS, 0, ends)

    key_pos = (c - REACH) * BLOCK + iota((WINDOW, WIDTH), 0)
    kaug[...] = jnp.where((starts <= key_pos) & (key_pos < ends), 1.0, 0.0).astype(BF16)
    row_pos = c * BLOCK + lax.shift_right_logical(iota((ROWS, WIDTH), 0), 3)
    outside = jnp.where((starts <= row_pos) & (row_pos < ends), 0.0, -FAR)
    qaug[...] = jnp.where(iota((ROWS, WIDTH), 1) <= NDOCS, outside, 0.0).astype(BF16)

    for t in range(TILES):
        g_t = jnp.transpose(g_ref[pl.ds(TILE * t, TILE), :])
        o_t = jnp.transpose(o_ref[pl.ds(TILE * t, TILE), :])
        gt[:, pl.ds(TILE * t, TILE)] = g_t
        delta[pl.ds(t, 1), :] = jnp.sum(
            g_t.astype(F32) * o_t.astype(F32), axis=0, keepdims=True
        )

    def ahead_by(window, i, o, other):
        return pltpu.make_async_remote_copy(
            src_ref=window.at[pl.ds(REACH * BLOCK, BLOCK)],
            dst_ref=window.at[pl.ds((REACH - o) * BLOCK, BLOCK)],
            send_sem=cs_sem.at[i, o // 2],
            recv_sem=cr_sem.at[i, o // 2],
            device_id={"ctx": other},
            device_id_type=MESH,
        )

    def aside(window, i, hop):
        at = (REACH - 2 * hop) * BLOCK - 2 * BLOCK * core
        return pltpu.make_async_remote_copy(
            src_ref=window.at[pl.ds(pl.multiple_of(at, BLOCK), BLOCK)],
            dst_ref=window.at[pl.ds((REACH - 2 * hop - 1) * BLOCK, BLOCK)],
            send_sem=cs_sem.at[i, 3 * hop],
            recv_sem=cr_sem.at[i, 3 * hop],
            device_id={"ctx": sib},
            device_id_type=MESH,
        )

    k_ahead = {o: ahead_by(kb, 0, o, ahead[o]) for o in (2, 4)}
    v_ahead = {o: ahead_by(vb, 1, o, ahead[o]) for o in (2, 4)}
    k_side = [aside(kb, 0, hop) for hop in range(2)]
    v_side = [aside(vb, 1, hop) for hop in range(2)]

    def scores(s):
        for t in range(TILES):
            lo, hi = reach(s, t)
            at = pl.ds(BLOCK * s + lo, hi - lo)
            here = pl.ds(TILE * t, TILE)
            left = jnp.concatenate([kb[at, :], kaug[at, :]], axis=1)
            right = jnp.concatenate([q_ref[here, :], qaug[here, :]], axis=1)
            x = dot(left, right, NT)
            if s == REACH:
                key = hi - HALF + iota((HALF, TILE), 0)
                query = STEP * t + lax.shift_right_logical(iota((HALF, TILE), 1), 3)
                own = jnp.where(key <= query, x[hi - HALF :], -1e30)
                x = own if hi == HALF else jnp.concatenate([x[:HALF], own], axis=0)
            m = jnp.max(x, axis=0, keepdims=True)
            e = jnp.exp2((x - m) * RATE)
            m_st[s, pl.ds(t, 1), :] = m
            l_st[s, pl.ds(t, 1), :] = jnp.sum(e, axis=0, keepdims=True)
            band[at, here] = e.astype(BF16)

    def relay_near(arrived, handed):
        arrived[2].wait_recv()

        @pl.when(core == 0)
        def _():
            handed[1].start()

        @pl.when(core == 1)
        def _():
            handed[0].start()

    def relay_far(arrived, handed):
        arrived[4].wait_recv()

        @pl.when(core == 1)
        def _():
            handed[1].start()

    for copy in k_copies:
        copy.wait_recv()
    for o in (2, 4):
        k_ahead[o].start()

    @pl.when(core == 0)
    def _():
        k_side[0].start()

    for copy in v_copies:
        copy.wait_recv()

    @pl.when(core == 0)
    def _():
        v_side[0].start()

    scores(4)
    for o in (2, 4):
        v_ahead[o].start()
    relay_near(k_ahead, k_side)
    scores(2)
    relay_far(k_ahead, k_side)
    scores(0)
    k_side[0].wait_recv()
    scores(3)
    k_side[1].wait_recv()
    scores(1)
    relay_near(v_ahead, v_side)

    slots = range(REACH + 1)
    top = functools.reduce(jnp.maximum, [m_st[s] for s in slots])
    parts = [jnp.exp2((m_st[s] - top) * RATE) for s in slots]
    total = sum(part * l_st[s] for s, part in enumerate(parts))
    for s, part in enumerate(parts):
        share = part / total
        w_st[s] = share
        wd_st[s] = share * delta[...]

    def value_grads(s):
        for t in range(TILES):
            here = pl.ds(TILE * t, TILE)
            gw[s, :, here] = (gt[:, here].astype(F32) * w_st[s, pl.ds(t, 1), :]).astype(BF16)
        for lo, hi, first, end in halves(s):
            at, rows = pl.ds(BLOCK * s + lo, hi - lo), pl.ds(first, end - first)
            dva[at, :] = dot(band[at, rows], gw[s, :, rows], NT)

    def key_grads(s):
        for t in range(TILES):
            lo, hi = reach(s, t)
            at = pl.ds(BLOCK * s + lo, hi - lo)
            here = pl.ds(TILE * t, TILE)
            dp = dot(vb[at, :], gw[s, :, here])
            band[at, here] = band[at, here] * (dp - wd_st[s, pl.ds(t, 1), :]).astype(BF16)
        for lo, hi, first, end in halves(s):
            at, rows = pl.ds(BLOCK * s + lo, hi - lo), pl.ds(first, end - first)
            dka[at, :] = dot(band[at, rows], q_ref[rows, :])

    def back(i, hop, other):
        return pltpu.make_async_remote_copy(
            src_ref=stage.at[i, hop],
            dst_ref=got.at[i, hop],
            send_sem=rs_sem.at[i, hop],
            recv_sem=rr_sem.at[i, hop],
            device_id={"ctx": other},
            device_id_type=MESH,
        )

    accs = (dva, dka)
    returns = [
        [back(i, hop, other) for hop, other in enumerate((sib, behind[1], behind[2], behind[4]))]
        for i in range(2)
    ]

    def hand(i, hop, s, extra):
        value = accs[i][pl.ds(BLOCK * s, BLOCK), :]
        if extra:
            value = value + got[i, 0].astype(F32)
        stage[i, hop] = value.astype(BF16)
        returns[i][hop].start()

    def sums(i):
        returns[i][0].wait_recv()

        @pl.when(core == 0)
        def _():
            hand(i, 2, 2, True)

        @pl.when(core == 1)
        def _():
            hand(i, 3, 0, True)

    def far_of_one(i):
        @pl.when(core == 1)
        def _():
            hand(i, 2, 2, False)

    def farther_of_zero(i):
        @pl.when(core == 0)
        def _():
            hand(i, 3, 0, False)

    last = []

    def finish(i):
        for hop in (3, 2, 1):
            returns[i][hop].wait_recv()
        whole = accs[i][pl.ds(REACH * BLOCK, BLOCK), :]
        for hop in (1, 2, 3):
            whole = whole + got[i, hop].astype(F32)
        if i == 1:
            whole = whole * SCALE
        sent[i] = whole.astype(BF16)
        for o, peer in enumerate(peers):
            copy = pltpu.make_async_remote_copy(
                src_ref=sent.at[i, pl.ds(pl.multiple_of(PIECE * peer, PIECE), PIECE)],
                dst_ref=fin_any.at[i, pl.ds(mine, PIECE)],
                send_sem=fs_sem.at[i, o],
                recv_sem=fr_sem.at[i, o],
                device_id={"head": peer},
                device_id_type=MESH,
            )
            copy.start()
            last.append(copy)
        save = pltpu.make_async_copy(
            sent.at[i, pl.ds(mine, PIECE)], fin_any.at[i, pl.ds(mine, PIECE)], out_sem.at[i]
        )
        save.start()
        saves.append(save)

    saves = []
    value_grads(0)
    farther_of_zero(0)
    value_grads(1)
    hand(0, 0, 1, False)
    relay_far(v_ahead, v_side)
    value_grads(2)
    far_of_one(0)
    value_grads(3)
    hand(0, 1, 3, False)
    sums(0)
    key_grads(0)
    farther_of_zero(1)
    v_side[1].wait_recv()
    key_grads(1)
    hand(1, 0, 1, False)
    key_grads(2)
    far_of_one(1)
    v_side[0].wait_recv()
    key_grads(3)
    hand(1, 1, 3, False)
    sums(1)
    value_grads(4)
    key_grads(4)
    finish(0)

    for t in range(TILES):
        here = pl.ds(TILE * t, TILE)
        first, end = reach(0, t)[0], REACH * BLOCK + reach(REACH, t)[1]
        at = pl.ds(first, end - first)
        dq_ref[here, :] = (dot(band[at, here], kb[at, :], TN) * SCALE).astype(BF16)

    save = pltpu.make_async_copy(dq_ref, dq_any, out_sem.at[2])
    save.start()
    saves.append(save)
    finish(1)

    for copy in last:
        copy.wait_recv()
    for copy in (*k_copies, *v_copies, *k_ahead.values(), *v_ahead.values(), *k_side, *v_side):
        copy.wait_send()
    for copy in (*returns[0], *returns[1], *last):
        copy.wait_send()
    for save in saves:
        save.wait()


PARTS = 1


def store(dq_any, fin_any, dq_out, dk_out, dv_out, dq_ref, fin, dk_ref, dv_ref, load_sem, save_sem):
    part = [pl.ds(ROWS // PARTS * i, ROWS // PARTS) for i in range(PARTS)]
    loads = [pltpu.make_async_copy(fin_any, fin, load_sem.at[PARTS])] + [
        pltpu.make_async_copy(dq_any.at[p], dq_ref.at[p], load_sem.at[i]) for i, p in enumerate(part)
    ]
    for load in loads:
        load.start()
    row, col = iota((BLOCK, BLOCK), 0), iota((BLOCK, BLOCK), 1)
    place = jnp.where(
        row == (col % PIECE) * GROUPS + col // PIECE, 1.0, 0.0
    ).astype(BF16)
    saves = []

    def save(source, target):
        copy = pltpu.make_async_copy(source, target, save_sem.at[len(saves)])
        copy.start()
        saves.append(copy)

    loads[0].wait()
    for i, (ref, out) in enumerate(((dv_ref, dv_out), (dk_ref, dk_out))):
        ref[...] = dot(place, fin[i]).astype(BF16)
        save(ref, out)
    for load, p in zip(loads[1:], part):
        load.wait()
        save(dq_ref.at[p], dq_out.at[p])
    for copy in saves:
        copy.wait()


def solution(mesh):
    n_ctx = mesh.shape["ctx"]
    dma = pltpu.SemaphoreType.DMA

    def body(queries, keys, values, output, grad_output, doc_lengths):
        flat = lambda x: x.reshape(-1, WIDTH)
        piece = PIECE * GROUPS
        dq, fin = pl.pallas_call(
            functools.partial(kernel, n_ctx),
            out_shape=(
                jax.ShapeDtypeStruct((ROWS, WIDTH), BF16),
                jax.ShapeDtypeStruct((2, piece, WIDTH), BF16),
            ),
            in_specs=[pl.BlockSpec(memory_space=pl.ANY)] * 6,
            out_specs=[pl.BlockSpec(memory_space=pl.ANY)] * 2,
            scratch_shapes=[
                pltpu.VMEM((ROWS, WIDTH), BF16),
                pltpu.SMEM((NDOCS,), jnp.int32),
                pltpu.VMEM((ROWS, WIDTH), BF16),
                pltpu.VMEM((ROWS, WIDTH), BF16),
                pltpu.VMEM((ROWS, WIDTH), BF16),
                pltpu.VMEM((piece, WIDTH), BF16),
                pltpu.VMEM((piece, WIDTH), BF16),
                pltpu.VMEM((WINDOW, WIDTH), BF16),
                pltpu.VMEM((WINDOW, WIDTH), BF16),
                pltpu.VMEM((BLOCK, BLOCK), BF16),
                pltpu.VMEM((piece, WIDTH), BF16),
                pltpu.VMEM((piece, WIDTH), BF16),
                pltpu.VMEM((WINDOW, WIDTH), BF16),
                pltpu.VMEM((ROWS, WIDTH), BF16),
                pltpu.VMEM((WIDTH, ROWS), BF16),
                pltpu.VMEM((TILES, TILE), F32),
                pltpu.VMEM((WINDOW, ROWS), BF16),
                pltpu.VMEM((REACH + 1, TILES, TILE), F32),
                pltpu.VMEM((REACH + 1, TILES, TILE), F32),
                pltpu.VMEM((REACH + 1, TILES, TILE), F32),
                pltpu.VMEM((REACH + 1, TILES, TILE), F32),
                pltpu.VMEM((REACH + 1, WIDTH, ROWS), BF16),
                pltpu.VMEM((WINDOW, WIDTH), F32),
                pltpu.VMEM((WINDOW, WIDTH), F32),
                pltpu.VMEM((2, 4, BLOCK, WIDTH), BF16),
                pltpu.VMEM((2, 4, BLOCK, WIDTH), BF16),
                pltpu.VMEM((2, BLOCK, WIDTH), BF16),
                dma((6,)),
                dma((3,)),
                dma((GROUPS - 1,)),
                dma((GROUPS - 1,)),
                dma((GROUPS - 1,)),
                dma((GROUPS - 1,)),
                dma((2, 4)),
                dma((2, 4)),
                dma((2, 4)),
                dma((2, 4)),
                dma((2, GROUPS - 1)),
                dma((2, GROUPS - 1)),
            ],
            compiler_params=pltpu.CompilerParams(
                collective_id=0, has_side_effects=True, vmem_limit_bytes=VMEM
            ),
        )(doc_lengths, flat(queries), flat(output), flat(grad_output), flat(keys), flat(values))
        dq, dk, dv = pl.pallas_call(
            store,
            out_shape=(
                jax.ShapeDtypeStruct((ROWS, WIDTH), BF16),
                jax.ShapeDtypeStruct((piece, WIDTH), BF16),
                jax.ShapeDtypeStruct((piece, WIDTH), BF16),
            ),
            in_specs=[pl.BlockSpec(memory_space=pl.ANY)] * 2,
            out_specs=[pl.BlockSpec(memory_space=pl.ANY)] * 3,
            scratch_shapes=[
                pltpu.VMEM((ROWS, WIDTH), BF16),
                pltpu.VMEM((2, piece, WIDTH), BF16),
                pltpu.VMEM((piece, WIDTH), BF16),
                pltpu.VMEM((piece, WIDTH), BF16),
                dma((PARTS + 1,)),
                dma((PARTS + 2,)),
            ],
            compiler_params=pltpu.CompilerParams(vmem_limit_bytes=VMEM),
        )(dq, fin)
        return (
            dq.reshape(queries.shape),
            dk.reshape(keys.shape),
            dv.reshape(values.shape),
        )

    return jax.shard_map(
        body,
        mesh=mesh,
        in_specs=(
            P("ctx", "head", None),
            P(("ctx", "head"), None, None),
            P(("ctx", "head"), None, None),
            P("ctx", "head", None),
            P("ctx", "head", None),
            P(),
        ),
        out_specs=(
            P("ctx", "head", None),
            P(("ctx", "head"), None, None),
            P(("ctx", "head"), None, None),
        ),
        check_vma=False,
    )
```

```python
import functools
import math

import jax
import jax.numpy as jnp
from jax import lax
from jax.experimental import pallas as pl
from jax.experimental.pallas import tpu as pltpu
from jax.sharding import PartitionSpec as P

MESH = pl.DeviceIdType.MESH
F32 = jnp.float32
BF16 = jnp.bfloat16

BLOCK = 256
REACH = 4
WINDOW = (REACH + 1) * BLOCK
WIDTH = 128
HEADS = 8
GROUPS = 8
ROWS = BLOCK * HEADS
TILE = 256
TILES = ROWS // TILE
STEP = TILE // HEADS
PIECE = BLOCK // GROUPS
NDOCS = 16
FAR = 2.0**20
SCALE = 1.0 / math.sqrt(WIDTH)
RATE = SCALE / math.log(2.0)

HALF = BLOCK // 2


def reach(s, t):
    if s == REACH:
        return (0, HALF) if t < TILES // 2 else (0, BLOCK)
    if s == 0 and t >= TILES // 2:
        return (HALF, BLOCK)
    return (0, BLOCK)


def halves(s):
    if s == REACH:
        return ((0, HALF, 0, ROWS), (HALF, BLOCK, ROWS // 2, ROWS))
    if s == 0:
        return ((0, HALF, 0, ROWS // 2), (HALF, BLOCK, 0, ROWS))
    return ((0, BLOCK, 0, ROWS),)


VMEM = (64 << 20) - (640 << 10)

NT = (((1,), (1,)), ((), ()))
NN = (((1,), (0,)), ((), ()))
TN = (((0,), (0,)), ((), ()))


def dot(a, b, dims=NN):
    return lax.dot_general(a, b, dims, preferred_element_type=F32)


def iota(shape, dim):
    return lax.broadcasted_iota(jnp.int32, shape, dim)


def kernel(
    n_ctx,
    lens_any, q_any, o_any, g_any, k_any, v_any,
    dq_any, fin_any,
    dq_ref, lens_ref, q_ref, o_ref, g_ref, k_ref, v_ref,
    kb, vb, order, kp, vp, kaug, qaug, gt, delta, band, m_st, l_st, w_st, wd_st,
    gw, dka, dva, stage, got, sent,
    in_sem, out_sem, ks_sem, kr_sem, vs_sem, vr_sem, cs_sem, cr_sem, rs_sem, rr_sem, fs_sem, fr_sem,
):
    c = lax.axis_index("ctx")
    z = lax.axis_index("head")
    core = lax.rem(c, 2)
    sib = c + 1 - 2 * core
    ahead = {o: lax.rem(c + o, n_ctx) for o in (1, 2, 4)}
    behind = {o: lax.rem(c + n_ctx - o, n_ctx) for o in (1, 2, 4)}
    peers = [lax.rem(z + o, GROUPS) for o in (4, 3, 5, 2, 6, 1, 7)]

    loads = []
    for i, (source, target) in enumerate(
        (
            (k_any, k_ref), (v_any, v_ref), (lens_any, lens_ref),
            (q_any, q_ref), (g_any, g_ref), (o_any, o_ref),
        )
    ):
        load = pltpu.make_async_copy(source, target, in_sem.at[i])
        loads.append(load)
    loads[0].start()
    loads[1].start()
    barrier = pltpu.get_barrier_semaphore()
    for peer in peers:
        pl.semaphore_signal(barrier, inc=1, device_id={"head": peer}, device_id_type=MESH)
    for other in (*ahead.values(), *behind.values()):
        pl.semaphore_signal(barrier, inc=1, device_id={"ctx": other}, device_id_type=MESH)

    for load in loads[2:]:
        load.start()
    row, col = iota((BLOCK, BLOCK), 0), iota((BLOCK, BLOCK), 1)
    order[...] = jnp.where(
        col == (row % PIECE) * GROUPS + row // PIECE, 1.0, 0.0
    ).astype(BF16)
    mine = pl.multiple_of(PIECE * z, PIECE)
    k_copies, v_copies = [], []
    for i, (given, piece, window, send, recv, copies) in enumerate(
        (
            (k_ref, kp, kb, ks_sem, kr_sem, k_copies),
            (v_ref, vp, vb, vs_sem, vr_sem, v_copies),
        )
    ):
        loads[i].wait()
        piece[...] = dot(order[...], given[...]).astype(BF16)
        if i == 0:
            pl.semaphore_wait(barrier, GROUPS - 1 + len(ahead) + len(behind))
        for o, peer in enumerate(peers):
            copy = pltpu.make_async_remote_copy(
                src_ref=piece.at[pl.ds(pl.multiple_of(PIECE * peer, PIECE), PIECE)],
                dst_ref=window.at[pl.ds(pl.multiple_of(REACH * BLOCK + mine, PIECE), PIECE)],
                send_sem=send.at[o],
                recv_sem=recv.at[o],
                device_id={"head": peer},
                device_id_type=MESH,
            )
            copy.start()
            copies.append(copy)
        window[pl.ds(pl.multiple_of(REACH * BLOCK + mine, PIECE), PIECE), :] = piece[pl.ds(mine, PIECE), :]

    for load in loads[2:]:
        load.wait()
    lane = iota((1, WIDTH), 1)
    start = jnp.int32(0)
    starts = jnp.full((1, WIDTH), 1 << 30, jnp.int32)
    ends = jnp.full((1, WIDTH), 1 << 30, jnp.int32)
    for doc in range(NDOCS):
        end = start + lens_ref[doc]
        starts = jnp.where(lane == doc, start, starts)
        ends = jnp.where(lane == doc, end, ends)
        start = end
    starts = jnp.where(lane == NDOCS, -(1 << 30), starts)
    ends = jnp.where(lane == NDOCS, 0, ends)

    key_pos = (c - REACH) * BLOCK + iota((WINDOW, WIDTH), 0)
    kaug[...] = jnp.where((starts <= key_pos) & (key_pos < ends), 1.0, 0.0).astype(BF16)
    row_pos = c * BLOCK + lax.shift_right_logical(iota((ROWS, WIDTH), 0), 3)
    outside = jnp.where((starts <= row_pos) & (row_pos < ends), 0.0, -FAR)
    qaug[...] = jnp.where(iota((ROWS, WIDTH), 1) <= NDOCS, outside, 0.0).astype(BF16)

    for t in range(TILES):
        g_t = jnp.transpose(g_ref[pl.ds(TILE * t, TILE), :])
        o_t = jnp.transpose(o_ref[pl.ds(TILE * t, TILE), :])
        gt[:, pl.ds(TILE * t, TILE)] = g_t
        delta[pl.ds(t, 1), :] = jnp.sum(
            g_t.astype(F32) * o_t.astype(F32), axis=0, keepdims=True
        )

    def ahead_by(window, i, o, other):
        return pltpu.make_async_remote_copy(
            src_ref=window.at[pl.ds(REACH * BLOCK, BLOCK)],
            dst_ref=window.at[pl.ds((REACH - o) * BLOCK, BLOCK)],
            send_sem=cs_sem.at[i, o // 2],
            recv_sem=cr_sem.at[i, o // 2],
            device_id={"ctx": other},
            device_id_type=MESH,
        )

    def aside(window, i, hop):
        at = (REACH - 2 * hop) * BLOCK - 2 * BLOCK * core
        return pltpu.make_async_remote_copy(
            src_ref=window.at[pl.ds(pl.multiple_of(at, BLOCK), BLOCK)],
            dst_ref=window.at[pl.ds((REACH - 2 * hop - 1) * BLOCK, BLOCK)],
            send_sem=cs_sem.at[i, 3 * hop],
            recv_sem=cr_sem.at[i, 3 * hop],
            device_id={"ctx": sib},
            device_id_type=MESH,
        )

    k_ahead = {o: ahead_by(kb, 0, o, ahead[o]) for o in (2, 4)}
    v_ahead = {o: ahead_by(vb, 1, o, ahead[o]) for o in (2, 4)}
    k_side = [aside(kb, 0, hop) for hop in range(2)]
    v_side = [aside(vb, 1, hop) for hop in range(2)]

    def scores(s):
        for t in range(TILES):
            lo, hi = reach(s, t)
            at = pl.ds(BLOCK * s + lo, hi - lo)
            here = pl.ds(TILE * t, TILE)
            left = jnp.concatenate([kb[at, :], kaug[at, :]], axis=1)
            right = jnp.concatenate([q_ref[here, :], qaug[here, :]], axis=1)
            x = dot(left, right, NT)
            if s == REACH:
                key = hi - HALF + iota((HALF, TILE), 0)
                query = STEP * t + lax.shift_right_logical(iota((HALF, TILE), 1), 3)
                own = jnp.where(key <= query, x[hi - HALF :], -1e30)
                x = own if hi == HALF else jnp.concatenate([x[:HALF], own], axis=0)
            m = jnp.max(x, axis=0, keepdims=True)
            e = jnp.exp2((x - m) * RATE)
            m_st[s, pl.ds(t, 1), :] = m
            l_st[s, pl.ds(t, 1), :] = jnp.sum(e, axis=0, keepdims=True)
            band[at, here] = e.astype(BF16)

    def relay_near(arrived, handed):
        arrived[2].wait_recv()

        @pl.when(core == 0)
        def _():
            handed[1].start()

        @pl.when(core == 1)
        def _():
            handed[0].start()

    def relay_far(arrived, handed):
        arrived[4].wait_recv()

        @pl.when(core == 1)
        def _():
            handed[1].start()

    for copy in k_copies:
        copy.wait_recv()
    for o in (2, 4):
        k_ahead[o].start()

    @pl.when(core == 0)
    def _():
        k_side[0].start()

    for copy in v_copies:
        copy.wait_recv()

    @pl.when(core == 0)
    def _():
        v_side[0].start()

    scores(4)
    v_ahead[2].start()
    relay_near(k_ahead, k_side)
    v_ahead[4].start()
    scores(2)
    relay_far(k_ahead, k_side)
    scores(0)
    k_side[0].wait_recv()
    scores(3)
    k_side[1].wait_recv()
    scores(1)
    relay_near(v_ahead, v_side)

    slots = range(REACH + 1)
    top = functools.reduce(jnp.maximum, [m_st[s] for s in slots])
    parts = [jnp.exp2((m_st[s] - top) * RATE) for s in slots]
    total = sum(part * l_st[s] for s, part in enumerate(parts))
    for s, part in enumerate(parts):
        share = part / total
        w_st[s] = share
        wd_st[s] = share * delta[...]

    def value_grads(s):
        for t in range(TILES):
            here = pl.ds(TILE * t, TILE)
            gw[s, :, here] = (gt[:, here].astype(F32) * w_st[s, pl.ds(t, 1), :]).astype(BF16)
        for lo, hi, first, end in halves(s):
            at, rows = pl.ds(BLOCK * s + lo, hi - lo), pl.ds(first, end - first)
            dva[at, :] = dot(band[at, rows], gw[s, :, rows], NT)

    def key_grads(s):
        for t in range(TILES):
            lo, hi = reach(s, t)
            at = pl.ds(BLOCK * s + lo, hi - lo)
            here = pl.ds(TILE * t, TILE)
            dp = dot(vb[at, :], gw[s, :, here])
            band[at, here] = band[at, here] * (dp - wd_st[s, pl.ds(t, 1), :]).astype(BF16)
        for lo, hi, first, end in halves(s):
            at, rows = pl.ds(BLOCK * s + lo, hi - lo), pl.ds(first, end - first)
            dka[at, :] = dot(band[at, rows], q_ref[rows, :])

    def back(i, hop, other):
        return pltpu.make_async_remote_copy(
            src_ref=stage.at[i, hop],
            dst_ref=got.at[i, hop],
            send_sem=rs_sem.at[i, hop],
            recv_sem=rr_sem.at[i, hop],
            device_id={"ctx": other},
            device_id_type=MESH,
        )

    accs = (dva, dka)
    returns = [
        [back(i, hop, other) for hop, other in enumerate((sib, behind[1], behind[2], behind[4]))]
        for i in range(2)
    ]

    def hand(i, hop, s, extra):
        value = accs[i][pl.ds(BLOCK * s, BLOCK), :]
        if extra:
            value = value + got[i, 0].astype(F32)
        stage[i, hop] = value.astype(BF16)
        returns[i][hop].start()

    def sums(i):
        returns[i][0].wait_recv()

        @pl.when(core == 0)
        def _():
            hand(i, 2, 2, True)

        @pl.when(core == 1)
        def _():
            hand(i, 3, 0, True)

    def far_of_one(i):
        @pl.when(core == 1)
        def _():
            hand(i, 2, 2, False)

    def farther_of_zero(i):
        @pl.when(core == 0)
        def _():
            hand(i, 3, 0, False)

    last = []

    def finish(i):
        for hop in (3, 2, 1):
            returns[i][hop].wait_recv()
        whole = accs[i][pl.ds(REACH * BLOCK, BLOCK), :]
        for hop in (1, 2, 3):
            whole = whole + got[i, hop].astype(F32)
        if i == 1:
            whole = whole * SCALE
        sent[i] = whole.astype(BF16)
        for o, peer in enumerate(peers):
            copy = pltpu.make_async_remote_copy(
                src_ref=sent.at[i, pl.ds(pl.multiple_of(PIECE * peer, PIECE), PIECE)],
                dst_ref=fin_any.at[i, pl.ds(mine, PIECE)],
                send_sem=fs_sem.at[i, o],
                recv_sem=fr_sem.at[i, o],
                device_id={"head": peer},
                device_id_type=MESH,
            )
            copy.start()
            last.append(copy)
        save = pltpu.make_async_copy(
            sent.at[i, pl.ds(mine, PIECE)], fin_any.at[i, pl.ds(mine, PIECE)], out_sem.at[i]
        )
        save.start()
        saves.append(save)

    saves = []
    value_grads(0)
    farther_of_zero(0)
    value_grads(1)
    hand(0, 0, 1, False)
    relay_far(v_ahead, v_side)
    value_grads(2)
    far_of_one(0)
    value_grads(3)
    hand(0, 1, 3, False)
    sums(0)
    key_grads(0)
    farther_of_zero(1)
    v_side[1].wait_recv()
    key_grads(1)
    hand(1, 0, 1, False)
    key_grads(2)
    far_of_one(1)
    v_side[0].wait_recv()
    key_grads(3)
    hand(1, 1, 3, False)
    sums(1)
    value_grads(4)
    key_grads(4)
    finish(0)

    for t in range(TILES):
        here = pl.ds(TILE * t, TILE)
        first, end = reach(0, t)[0], REACH * BLOCK + reach(REACH, t)[1]
        at = pl.ds(first, end - first)
        dq_ref[here, :] = (dot(band[at, here], kb[at, :], TN) * SCALE).astype(BF16)

    save = pltpu.make_async_copy(dq_ref, dq_any, out_sem.at[2])
    save.start()
    saves.append(save)
    finish(1)

    for copy in last:
        copy.wait_recv()
    for copy in (*k_copies, *v_copies, *k_ahead.values(), *v_ahead.values(), *k_side, *v_side):
        copy.wait_send()
    for copy in (*returns[0], *returns[1], *last):
        copy.wait_send()
    for save in saves:
        save.wait()


PARTS = 1


def store(dq_any, fin_any, dq_out, dk_out, dv_out, dq_ref, fin, dk_ref, dv_ref, load_sem, save_sem):
    part = [pl.ds(ROWS // PARTS * i, ROWS // PARTS) for i in range(PARTS)]
    loads = [pltpu.make_async_copy(fin_any, fin, load_sem.at[PARTS])] + [
        pltpu.make_async_copy(dq_any.at[p], dq_ref.at[p], load_sem.at[i]) for i, p in enumerate(part)
    ]
    for load in loads:
        load.start()
    row, col = iota((BLOCK, BLOCK), 0), iota((BLOCK, BLOCK), 1)
    place = jnp.where(
        row == (col % PIECE) * GROUPS + col // PIECE, 1.0, 0.0
    ).astype(BF16)
    saves = []

    def save(source, target):
        copy = pltpu.make_async_copy(source, target, save_sem.at[len(saves)])
        copy.start()
        saves.append(copy)

    loads[0].wait()
    for i, (ref, out) in enumerate(((dv_ref, dv_out), (dk_ref, dk_out))):
        ref[...] = dot(place, fin[i]).astype(BF16)
        save(ref, out)
    for load, p in zip(loads[1:], part):
        load.wait()
        save(dq_ref.at[p], dq_out.at[p])
    for copy in saves:
        copy.wait()


def solution(mesh):
    n_ctx = mesh.shape["ctx"]
    dma = pltpu.SemaphoreType.DMA

    def body(queries, keys, values, output, grad_output, doc_lengths):
        flat = lambda x: x.reshape(-1, WIDTH)
        piece = PIECE * GROUPS
        dq, fin = pl.pallas_call(
            functools.partial(kernel, n_ctx),
            out_shape=(
                jax.ShapeDtypeStruct((ROWS, WIDTH), BF16),
                jax.ShapeDtypeStruct((2, piece, WIDTH), BF16),
            ),
            in_specs=[pl.BlockSpec(memory_space=pl.ANY)] * 6,
            out_specs=[pl.BlockSpec(memory_space=pl.ANY)] * 2,
            scratch_shapes=[
                pltpu.VMEM((ROWS, WIDTH), BF16),
                pltpu.SMEM((NDOCS,), jnp.int32),
                pltpu.VMEM((ROWS, WIDTH), BF16),
                pltpu.VMEM((ROWS, WIDTH), BF16),
                pltpu.VMEM((ROWS, WIDTH), BF16),
                pltpu.VMEM((piece, WIDTH), BF16),
                pltpu.VMEM((piece, WIDTH), BF16),
                pltpu.VMEM((WINDOW, WIDTH), BF16),
                pltpu.VMEM((WINDOW, WIDTH), BF16),
                pltpu.VMEM((BLOCK, BLOCK), BF16),
                pltpu.VMEM((piece, WIDTH), BF16),
                pltpu.VMEM((piece, WIDTH), BF16),
                pltpu.VMEM((WINDOW, WIDTH), BF16),
                pltpu.VMEM((ROWS, WIDTH), BF16),
                pltpu.VMEM((WIDTH, ROWS), BF16),
                pltpu.VMEM((TILES, TILE), F32),
                pltpu.VMEM((WINDOW, ROWS), BF16),
                pltpu.VMEM((REACH + 1, TILES, TILE), F32),
                pltpu.VMEM((REACH + 1, TILES, TILE), F32),
                pltpu.VMEM((REACH + 1, TILES, TILE), F32),
                pltpu.VMEM((REACH + 1, TILES, TILE), F32),
                pltpu.VMEM((REACH + 1, WIDTH, ROWS), BF16),
                pltpu.VMEM((WINDOW, WIDTH), F32),
                pltpu.VMEM((WINDOW, WIDTH), F32),
                pltpu.VMEM((2, 4, BLOCK, WIDTH), BF16),
                pltpu.VMEM((2, 4, BLOCK, WIDTH), BF16),
                pltpu.VMEM((2, BLOCK, WIDTH), BF16),
                dma((6,)),
                dma((3,)),
                dma((GROUPS - 1,)),
                dma((GROUPS - 1,)),
                dma((GROUPS - 1,)),
                dma((GROUPS - 1,)),
                dma((2, 4)),
                dma((2, 4)),
                dma((2, 4)),
                dma((2, 4)),
                dma((2, GROUPS - 1)),
                dma((2, GROUPS - 1)),
            ],
            compiler_params=pltpu.CompilerParams(
                collective_id=0, has_side_effects=True, vmem_limit_bytes=VMEM
            ),
        )(doc_lengths, flat(queries), flat(output), flat(grad_output), flat(keys), flat(values))
        dq, dk, dv = pl.pallas_call(
            store,
            out_shape=(
                jax.ShapeDtypeStruct((ROWS, WIDTH), BF16),
                jax.ShapeDtypeStruct((piece, WIDTH), BF16),
                jax.ShapeDtypeStruct((piece, WIDTH), BF16),
            ),
            in_specs=[pl.BlockSpec(memory_space=pl.ANY)] * 2,
            out_specs=[pl.BlockSpec(memory_space=pl.ANY)] * 3,
            scratch_shapes=[
                pltpu.VMEM((ROWS, WIDTH), BF16),
                pltpu.VMEM((2, piece, WIDTH), BF16),
                pltpu.VMEM((piece, WIDTH), BF16),
                pltpu.VMEM((piece, WIDTH), BF16),
                dma((PARTS + 1,)),
                dma((PARTS + 2,)),
            ],
            compiler_params=pltpu.CompilerParams(vmem_limit_bytes=VMEM),
        )(dq, fin)
        return (
            dq.reshape(queries.shape),
            dk.reshape(keys.shape),
            dv.reshape(values.shape),
        )

    return jax.shard_map(
        body,
        mesh=mesh,
        in_specs=(
            P("ctx", "head", None),
            P(("ctx", "head"), None, None),
            P(("ctx", "head"), None, None),
            P("ctx", "head", None),
            P("ctx", "head", None),
            P(),
        ),
        out_specs=(
            P("ctx", "head", None),
            P(("ctx", "head"), None, None),
            P(("ctx", "head"), None, None),
        ),
        check_vma=False,
    )
```

```python
import functools
import math

import jax
import jax.numpy as jnp
from jax import lax
from jax.experimental import pallas as pl
from jax.experimental.pallas import tpu as pltpu
from jax.sharding import PartitionSpec as P

MESH = pl.DeviceIdType.MESH
F32 = jnp.float32
BF16 = jnp.bfloat16

BLOCK = 256
REACH = 4
WINDOW = (REACH + 1) * BLOCK
WIDTH = 128
HEADS = 8
GROUPS = 8
ROWS = BLOCK * HEADS
TILE = 256
TILES = ROWS // TILE
STEP = TILE // HEADS
PIECE = BLOCK // GROUPS
NDOCS = 16
FAR = 2.0**20
SCALE = 1.0 / math.sqrt(WIDTH)
RATE = SCALE / math.log(2.0)

HALF = BLOCK // 2


def reach(s, t):
    if s == REACH:
        return (0, HALF) if t < TILES // 2 else (0, BLOCK)
    if s == 0 and t >= TILES // 2:
        return (HALF, BLOCK)
    return (0, BLOCK)


def halves(s):
    if s == REACH:
        return ((0, HALF, 0, ROWS), (HALF, BLOCK, ROWS // 2, ROWS))
    if s == 0:
        return ((0, HALF, 0, ROWS // 2), (HALF, BLOCK, 0, ROWS))
    return ((0, BLOCK, 0, ROWS),)


VMEM = (64 << 20) - (640 << 10)

NT = (((1,), (1,)), ((), ()))
NN = (((1,), (0,)), ((), ()))
TN = (((0,), (0,)), ((), ()))


def dot(a, b, dims=NN):
    return lax.dot_general(a, b, dims, preferred_element_type=F32)


def iota(shape, dim):
    return lax.broadcasted_iota(jnp.int32, shape, dim)


def kernel(
    n_ctx,
    lens_any, q_any, o_any, g_any, k_any, v_any,
    dq_any, fin_any,
    dq_ref, lens_ref, q_ref, o_ref, g_ref, k_ref, v_ref,
    kb, vb, order, kp, vp, kaug, qaug, gt, delta, band, m_st, l_st, w_st, wd_st,
    gw, dka, dva, stage, got, sent,
    in_sem, out_sem, ks_sem, kr_sem, vs_sem, vr_sem, cs_sem, cr_sem, rs_sem, rr_sem, fs_sem, fr_sem,
):
    c = lax.axis_index("ctx")
    z = lax.axis_index("head")
    core = lax.rem(c, 2)
    sib = c + 1 - 2 * core
    ahead = {o: lax.rem(c + o, n_ctx) for o in (1, 2, 4)}
    behind = {o: lax.rem(c + n_ctx - o, n_ctx) for o in (1, 2, 4)}
    peers = [lax.rem(z + o, GROUPS) for o in (4, 3, 5, 2, 6, 1, 7)]

    loads = []
    for i, (source, target) in enumerate(
        (
            (k_any, k_ref), (v_any, v_ref), (lens_any, lens_ref),
            (q_any, q_ref), (g_any, g_ref), (o_any, o_ref),
        )
    ):
        load = pltpu.make_async_copy(source, target, in_sem.at[i])
        loads.append(load)
    loads[0].start()
    loads[1].start()
    barrier = pltpu.get_barrier_semaphore()
    for peer in peers:
        pl.semaphore_signal(barrier, inc=1, device_id={"head": peer}, device_id_type=MESH)
    for other in (*ahead.values(), *behind.values()):
        pl.semaphore_signal(barrier, inc=1, device_id={"ctx": other}, device_id_type=MESH)

    for load in loads[2:]:
        load.start()
    row, col = iota((BLOCK, BLOCK), 0), iota((BLOCK, BLOCK), 1)
    order[...] = jnp.where(
        col == (row % PIECE) * GROUPS + row // PIECE, 1.0, 0.0
    ).astype(BF16)
    mine = pl.multiple_of(PIECE * z, PIECE)
    k_copies, v_copies = [], []
    for i, (given, piece, window, send, recv, copies) in enumerate(
        (
            (k_ref, kp, kb, ks_sem, kr_sem, k_copies),
            (v_ref, vp, vb, vs_sem, vr_sem, v_copies),
        )
    ):
        loads[i].wait()
        piece[...] = dot(order[...], given[...]).astype(BF16)
        if i == 0:
            pl.semaphore_wait(barrier, GROUPS - 1 + len(ahead) + len(behind))
        for o, peer in enumerate(peers):
            copy = pltpu.make_async_remote_copy(
                src_ref=piece.at[pl.ds(pl.multiple_of(PIECE * peer, PIECE), PIECE)],
                dst_ref=window.at[pl.ds(pl.multiple_of(REACH * BLOCK + mine, PIECE), PIECE)],
                send_sem=send.at[o],
                recv_sem=recv.at[o],
                device_id={"head": peer},
                device_id_type=MESH,
            )
            copy.start()
            copies.append(copy)
        window[pl.ds(pl.multiple_of(REACH * BLOCK + mine, PIECE), PIECE), :] = piece[pl.ds(mine, PIECE), :]

    for load in loads[2:]:
        load.wait()
    lane = iota((1, WIDTH), 1)
    start = jnp.int32(0)
    starts = jnp.full((1, WIDTH), 1 << 30, jnp.int32)
    ends = jnp.full((1, WIDTH), 1 << 30, jnp.int32)
    for doc in range(NDOCS):
        end = start + lens_ref[doc]
        starts = jnp.where(lane == doc, start, starts)
        ends = jnp.where(lane == doc, end, ends)
        start = end
    starts = jnp.where(lane == NDOCS, -(1 << 30), starts)
    ends = jnp.where(lane == NDOCS, 0, ends)

    key_pos = (c - REACH) * BLOCK + iota((WINDOW, WIDTH), 0)
    kaug[...] = jnp.where((starts <= key_pos) & (key_pos < ends), 1.0, 0.0).astype(BF16)
    row_pos = c * BLOCK + lax.shift_right_logical(iota((ROWS, WIDTH), 0), 3)
    outside = jnp.where((starts <= row_pos) & (row_pos < ends), 0.0, -FAR)
    qaug[...] = jnp.where(iota((ROWS, WIDTH), 1) <= NDOCS, outside, 0.0).astype(BF16)

    for t in range(TILES):
        g_t = jnp.transpose(g_ref[pl.ds(TILE * t, TILE), :])
        o_t = jnp.transpose(o_ref[pl.ds(TILE * t, TILE), :])
        gt[:, pl.ds(TILE * t, TILE)] = g_t
        delta[pl.ds(t, 1), :] = jnp.sum(
            g_t.astype(F32) * o_t.astype(F32), axis=0, keepdims=True
        )

    def ahead_by(window, i, o, other):
        return pltpu.make_async_remote_copy(
            src_ref=window.at[pl.ds(REACH * BLOCK, BLOCK)],
            dst_ref=window.at[pl.ds((REACH - o) * BLOCK, BLOCK)],
            send_sem=cs_sem.at[i, o // 2],
            recv_sem=cr_sem.at[i, o // 2],
            device_id={"ctx": other},
            device_id_type=MESH,
        )

    def aside(window, i, hop):
        at = (REACH - 2 * hop) * BLOCK - 2 * BLOCK * core
        return pltpu.make_async_remote_copy(
            src_ref=window.at[pl.ds(pl.multiple_of(at, BLOCK), BLOCK)],
            dst_ref=window.at[pl.ds((REACH - 2 * hop - 1) * BLOCK, BLOCK)],
            send_sem=cs_sem.at[i, 3 * hop],
            recv_sem=cr_sem.at[i, 3 * hop],
            device_id={"ctx": sib},
            device_id_type=MESH,
        )

    k_ahead = {o: ahead_by(kb, 0, o, ahead[o]) for o in (2, 4)}
    v_ahead = {o: ahead_by(vb, 1, o, ahead[o]) for o in (2, 4)}
    k_side = [aside(kb, 0, hop) for hop in range(2)]
    v_side = [aside(vb, 1, hop) for hop in range(2)]

    def scores(s):
        for t in range(TILES):
            lo, hi = reach(s, t)
            at = pl.ds(BLOCK * s + lo, hi - lo)
            here = pl.ds(TILE * t, TILE)
            left = jnp.concatenate([kb[at, :], kaug[at, :]], axis=1)
            right = jnp.concatenate([q_ref[here, :], qaug[here, :]], axis=1)
            x = dot(left, right, NT)
            if s == REACH:
                key = hi - HALF + iota((HALF, TILE), 0)
                query = STEP * t + lax.shift_right_logical(iota((HALF, TILE), 1), 3)
                own = jnp.where(key <= query, x[hi - HALF :], -1e30)
                x = own if hi == HALF else jnp.concatenate([x[:HALF], own], axis=0)
            m = jnp.max(x, axis=0, keepdims=True)
            e = jnp.exp2((x - m) * RATE)
            m_st[s, pl.ds(t, 1), :] = m
            l_st[s, pl.ds(t, 1), :] = jnp.sum(e, axis=0, keepdims=True)
            band[at, here] = e.astype(BF16)

    def relay_near(arrived, handed):
        arrived[2].wait_recv()

        @pl.when(core == 0)
        def _():
            handed[1].start()

        @pl.when(core == 1)
        def _():
            handed[0].start()

    def relay_far(arrived, handed):
        arrived[4].wait_recv()

        @pl.when(core == 1)
        def _():
            handed[1].start()

    for copy in k_copies:
        copy.wait_recv()
    for o in (4, 2):
        k_ahead[o].start()

    @pl.when(core == 0)
    def _():
        k_side[0].start()

    for copy in v_copies:
        copy.wait_recv()

    @pl.when(core == 0)
    def _():
        v_side[0].start()

    scores(4)
    v_ahead[2].start()
    relay_near(k_ahead, k_side)
    v_ahead[4].start()
    scores(2)
    relay_far(k_ahead, k_side)
    scores(0)
    k_side[0].wait_recv()
    scores(3)
    k_side[1].wait_recv()
    scores(1)
    relay_near(v_ahead, v_side)

    slots = range(REACH + 1)
    top = functools.reduce(jnp.maximum, [m_st[s] for s in slots])
    parts = [jnp.exp2((m_st[s] - top) * RATE) for s in slots]
    total = sum(part * l_st[s] for s, part in enumerate(parts))
    for s, part in enumerate(parts):
        share = part / total
        w_st[s] = share
        wd_st[s] = share * delta[...]

    def value_grads(s):
        for t in range(TILES):
            here = pl.ds(TILE * t, TILE)
            gw[s, :, here] = (gt[:, here].astype(F32) * w_st[s, pl.ds(t, 1), :]).astype(BF16)
        for lo, hi, first, end in halves(s):
            at, rows = pl.ds(BLOCK * s + lo, hi - lo), pl.ds(first, end - first)
            dva[at, :] = dot(band[at, rows], gw[s, :, rows], NT)

    def key_grads(s):
        for t in range(TILES):
            lo, hi = reach(s, t)
            at = pl.ds(BLOCK * s + lo, hi - lo)
            here = pl.ds(TILE * t, TILE)
            dp = dot(vb[at, :], gw[s, :, here])
            band[at, here] = band[at, here] * (dp - wd_st[s, pl.ds(t, 1), :]).astype(BF16)
        for lo, hi, first, end in halves(s):
            at, rows = pl.ds(BLOCK * s + lo, hi - lo), pl.ds(first, end - first)
            dka[at, :] = dot(band[at, rows], q_ref[rows, :])

    def back(i, hop, other):
        return pltpu.make_async_remote_copy(
            src_ref=stage.at[i, hop],
            dst_ref=got.at[i, hop],
            send_sem=rs_sem.at[i, hop],
            recv_sem=rr_sem.at[i, hop],
            device_id={"ctx": other},
            device_id_type=MESH,
        )

    accs = (dva, dka)
    returns = [
        [back(i, hop, other) for hop, other in enumerate((sib, behind[1], behind[2], behind[4]))]
        for i in range(2)
    ]

    def hand(i, hop, s, extra):
        value = accs[i][pl.ds(BLOCK * s, BLOCK), :]
        if extra:
            value = value + got[i, 0].astype(F32)
        stage[i, hop] = value.astype(BF16)
        returns[i][hop].start()

    def sums(i):
        returns[i][0].wait_recv()

        @pl.when(core == 0)
        def _():
            hand(i, 2, 2, True)

        @pl.when(core == 1)
        def _():
            hand(i, 3, 0, True)

    def far_of_one(i):
        @pl.when(core == 1)
        def _():
            hand(i, 2, 2, False)

    def farther_of_zero(i):
        @pl.when(core == 0)
        def _():
            hand(i, 3, 0, False)

    last = []

    def finish(i):
        for hop in (3, 2, 1):
            returns[i][hop].wait_recv()
        whole = accs[i][pl.ds(REACH * BLOCK, BLOCK), :]
        for hop in (1, 2, 3):
            whole = whole + got[i, hop].astype(F32)
        if i == 1:
            whole = whole * SCALE
        sent[i] = whole.astype(BF16)
        for o, peer in enumerate(peers):
            copy = pltpu.make_async_remote_copy(
                src_ref=sent.at[i, pl.ds(pl.multiple_of(PIECE * peer, PIECE), PIECE)],
                dst_ref=fin_any.at[i, pl.ds(mine, PIECE)],
                send_sem=fs_sem.at[i, o],
                recv_sem=fr_sem.at[i, o],
                device_id={"head": peer},
                device_id_type=MESH,
            )
            copy.start()
            last.append(copy)
        save = pltpu.make_async_copy(
            sent.at[i, pl.ds(mine, PIECE)], fin_any.at[i, pl.ds(mine, PIECE)], out_sem.at[i]
        )
        save.start()
        saves.append(save)

    saves = []
    value_grads(0)
    farther_of_zero(0)
    value_grads(1)
    hand(0, 0, 1, False)
    relay_far(v_ahead, v_side)
    value_grads(2)
    far_of_one(0)
    value_grads(3)
    hand(0, 1, 3, False)
    sums(0)
    key_grads(0)
    farther_of_zero(1)
    v_side[1].wait_recv()
    key_grads(1)
    hand(1, 0, 1, False)
    key_grads(2)
    far_of_one(1)
    v_side[0].wait_recv()
    key_grads(3)
    hand(1, 1, 3, False)
    sums(1)
    value_grads(4)
    key_grads(4)
    finish(0)

    for t in range(TILES):
        here = pl.ds(TILE * t, TILE)
        first, end = reach(0, t)[0], REACH * BLOCK + reach(REACH, t)[1]
        at = pl.ds(first, end - first)
        dq_ref[here, :] = (dot(band[at, here], kb[at, :], TN) * SCALE).astype(BF16)

    save = pltpu.make_async_copy(dq_ref, dq_any, out_sem.at[2])
    save.start()
    saves.append(save)
    finish(1)

    for copy in last:
        copy.wait_recv()
    for copy in (*k_copies, *v_copies, *k_ahead.values(), *v_ahead.values(), *k_side, *v_side):
        copy.wait_send()
    for copy in (*returns[0], *returns[1], *last):
        copy.wait_send()
    for save in saves:
        save.wait()


PARTS = 1


def store(dq_any, fin_any, dq_out, dk_out, dv_out, dq_ref, fin, dk_ref, dv_ref, load_sem, save_sem):
    part = [pl.ds(ROWS // PARTS * i, ROWS // PARTS) for i in range(PARTS)]
    loads = [pltpu.make_async_copy(fin_any, fin, load_sem.at[PARTS])] + [
        pltpu.make_async_copy(dq_any.at[p], dq_ref.at[p], load_sem.at[i]) for i, p in enumerate(part)
    ]
    for load in loads:
        load.start()
    row, col = iota((BLOCK, BLOCK), 0), iota((BLOCK, BLOCK), 1)
    place = jnp.where(
        row == (col % PIECE) * GROUPS + col // PIECE, 1.0, 0.0
    ).astype(BF16)
    saves = []

    def save(source, target):
        copy = pltpu.make_async_copy(source, target, save_sem.at[len(saves)])
        copy.start()
        saves.append(copy)

    loads[0].wait()
    for i, (ref, out) in enumerate(((dv_ref, dv_out), (dk_ref, dk_out))):
        ref[...] = dot(place, fin[i]).astype(BF16)
        save(ref, out)
    for load, p in zip(loads[1:], part):
        load.wait()
        save(dq_ref.at[p], dq_out.at[p])
    for copy in saves:
        copy.wait()


def solution(mesh):
    n_ctx = mesh.shape["ctx"]
    dma = pltpu.SemaphoreType.DMA

    def body(queries, keys, values, output, grad_output, doc_lengths):
        flat = lambda x: x.reshape(-1, WIDTH)
        piece = PIECE * GROUPS
        dq, fin = pl.pallas_call(
            functools.partial(kernel, n_ctx),
            out_shape=(
                jax.ShapeDtypeStruct((ROWS, WIDTH), BF16),
                jax.ShapeDtypeStruct((2, piece, WIDTH), BF16),
            ),
            in_specs=[pl.BlockSpec(memory_space=pl.ANY)] * 6,
            out_specs=[pl.BlockSpec(memory_space=pl.ANY)] * 2,
            scratch_shapes=[
                pltpu.VMEM((ROWS, WIDTH), BF16),
                pltpu.SMEM((NDOCS,), jnp.int32),
                pltpu.VMEM((ROWS, WIDTH), BF16),
                pltpu.VMEM((ROWS, WIDTH), BF16),
                pltpu.VMEM((ROWS, WIDTH), BF16),
                pltpu.VMEM((piece, WIDTH), BF16),
                pltpu.VMEM((piece, WIDTH), BF16),
                pltpu.VMEM((WINDOW, WIDTH), BF16),
                pltpu.VMEM((WINDOW, WIDTH), BF16),
                pltpu.VMEM((BLOCK, BLOCK), BF16),
                pltpu.VMEM((piece, WIDTH), BF16),
                pltpu.VMEM((piece, WIDTH), BF16),
                pltpu.VMEM((WINDOW, WIDTH), BF16),
                pltpu.VMEM((ROWS, WIDTH), BF16),
                pltpu.VMEM((WIDTH, ROWS), BF16),
                pltpu.VMEM((TILES, TILE), F32),
                pltpu.VMEM((WINDOW, ROWS), BF16),
                pltpu.VMEM((REACH + 1, TILES, TILE), F32),
                pltpu.VMEM((REACH + 1, TILES, TILE), F32),
                pltpu.VMEM((REACH + 1, TILES, TILE), F32),
                pltpu.VMEM((REACH + 1, TILES, TILE), F32),
                pltpu.VMEM((REACH + 1, WIDTH, ROWS), BF16),
                pltpu.VMEM((WINDOW, WIDTH), F32),
                pltpu.VMEM((WINDOW, WIDTH), F32),
                pltpu.VMEM((2, 4, BLOCK, WIDTH), BF16),
                pltpu.VMEM((2, 4, BLOCK, WIDTH), BF16),
                pltpu.VMEM((2, BLOCK, WIDTH), BF16),
                dma((6,)),
                dma((3,)),
                dma((GROUPS - 1,)),
                dma((GROUPS - 1,)),
                dma((GROUPS - 1,)),
                dma((GROUPS - 1,)),
                dma((2, 4)),
                dma((2, 4)),
                dma((2, 4)),
                dma((2, 4)),
                dma((2, GROUPS - 1)),
                dma((2, GROUPS - 1)),
            ],
            compiler_params=pltpu.CompilerParams(
                collective_id=0, has_side_effects=True, vmem_limit_bytes=VMEM
            ),
        )(doc_lengths, flat(queries), flat(output), flat(grad_output), flat(keys), flat(values))
        dq, dk, dv = pl.pallas_call(
            store,
            out_shape=(
                jax.ShapeDtypeStruct((ROWS, WIDTH), BF16),
                jax.ShapeDtypeStruct((piece, WIDTH), BF16),
                jax.ShapeDtypeStruct((piece, WIDTH), BF16),
            ),
            in_specs=[pl.BlockSpec(memory_space=pl.ANY)] * 2,
            out_specs=[pl.BlockSpec(memory_space=pl.ANY)] * 3,
            scratch_shapes=[
                pltpu.VMEM((ROWS, WIDTH), BF16),
                pltpu.VMEM((2, piece, WIDTH), BF16),
                pltpu.VMEM((piece, WIDTH), BF16),
                pltpu.VMEM((piece, WIDTH), BF16),
                dma((PARTS + 1,)),
                dma((PARTS + 2,)),
            ],
            compiler_params=pltpu.CompilerParams(vmem_limit_bytes=VMEM),
        )(dq, fin)
        return (
            dq.reshape(queries.shape),
            dk.reshape(keys.shape),
            dv.reshape(values.shape),
        )

    return jax.shard_map(
        body,
        mesh=mesh,
        in_specs=(
            P("ctx", "head", None),
            P(("ctx", "head"), None, None),
            P(("ctx", "head"), None, None),
            P("ctx", "head", None),
            P("ctx", "head", None),
            P(),
        ),
        out_specs=(
            P("ctx", "head", None),
            P(("ctx", "head"), None, None),
            P(("ctx", "head"), None, None),
        ),
        check_vma=False,
    )
```
